256 devices in a mesh: nodes: 64 (over z, y, core), chaos: 4 (over x).
Axes of the slice: x: 4, y: 4, z: 8, core: 2. Of those that a mesh axis runs over, the one named last changes fastest.
Arguments:
- right_side: float32 [120, 262144], P('chaos', 'nodes'), may hold values from -6 to 6
- diag_blocks: float32 [4096, 4096], P('nodes')
- off_blocks: float32 [4096, 4, 4096], P('nodes'), may hold values from -3 to 3
- smoother: float32 [4096, 4096], P('nodes')
- col_index: int32 [4096, 4], P('nodes'), may hold values from 0 to 79
- send_list: int32 [1024], P('nodes'), may hold values from 0 to 63
- agg_map: int32 [262144], P('nodes'), may hold values from 0 to 255
- owner_map: int32 [16384, 1], P('nodes'), may hold values from 0 to 15; in each aligned block of 256 rows (0 to 255, 256 to 511, ...) at most 20 rows name the same one
- coarse_diag: float32 [16384], P('nodes'), may hold values from 1 to 4
- coarse_weight: float32 [16384], P('nodes'), may hold values from 0.0001953125 to 0.001953125
- coarse_gain: float32 [16384], P('nodes'), may hold values from 0.2 to 2
Outputs:
- solution_field: float32 [120, 262144], P('chaos', 'nodes')
- residual_ratio: float32 [], replicated
The draws below stay inside these ranges and needn't reach their ends.
Inputs may be any that keep to these rules, and one draw needn't show every extreme that they name: `owner_map`: no owner gets more than 20 aggregates of one device; on some device one owner gets exactly 20. `send_list`: the first 8 entries of a device are blocks its previous device reads, the last 8 those its next device reads.
All inputs are finite; a program needn't handle non-finite values.
Results may differ from the reference program's by a relative error of at most 0.0003.
Values sent between devices are 32-bit elements; how exact they have to be, the bound alone decides.
A program may use at most 128 MiB of HBM per device.

```python
import math
import jax
import jax.numpy as jnp
import numpy as np
from jax import lax

P_SIZE = 120
NB_DEV = 64
H = 8
KB = 4
CSWEEPS = 3
NA_DEV = 256
NB_TOTAL = 4096
NODES = 262144
NA_TOTAL = 16384
NOWN = 16
CAP = 20
N_NODES = 64


def draw_diag_blocks(key, part):
    key = jax.random.fold_in(key, 11)
    eye = jnp.eye(64, dtype=jnp.float32)
    noise = 0.3 * jax.random.normal(key, (NB_TOTAL, 64, 64), jnp.float32)
    return (8.0 * eye + noise).reshape(NB_TOTAL, 4096)


def draw_smoother(key, part):
    key = jax.random.fold_in(key, 23)
    eye = jnp.eye(64, dtype=jnp.float32)
    noise = 0.012 * jax.random.normal(key, (NB_TOTAL, 64, 64), jnp.float32)
    return (0.1 * eye + noise).reshape(NB_TOTAL, 4096)


def plant(entries, rng, smallest, top_value):
    spot = [jax.random.randint(jax.random.fold_in(rng, axis), (), 0, length) for axis, length in enumerate(entries.shape)]
    longest = entries.shape.index(max(entries.shape))
    next_to = spot[:longest] + [(spot[longest] + 1) % entries.shape[longest]] + spot[longest + 1:]
    return entries.at[tuple(spot)].set(smallest).at[tuple(next_to)].set(top_value)


def steps_of(rng, extent, cuts, smallest, largest):
    def one(position, parts):
        draws = jax.random.uniform(jax.random.fold_in(jax.random.fold_in(rng, 6), position), (parts,), jnp.float32, smallest / len(cuts), largest / len(cuts))
        return jnp.repeat(jnp.exp(draws), extent[position] // parts).reshape((-1,) + (1,) * (len(extent) - position - 1))

    factor_of = one(*cuts[0])
    for cut in cuts[1:]:
        factor_of = factor_of * one(*cut)
    return factor_of


def shared_out(own_key, own, number, rows, amount, top, reach, slope):
    ranking = jax.random.permutation(own_key, amount)
    heavy_load, common = load_shares(amount, rows * top, reach, slope, True), load_shares(amount, rows * top, reach, slope, False)
    places = jnp.arange(amount)

    def named(tallies, offset_by):
        used = int((tallies > 0).sum())
        fixed = max(1, used // 4)
        passed = fixed + (places - fixed + offset_by * (used - fixed)) % max(1, amount - fixed)
        return jnp.zeros((amount,), jnp.int32).at[ranking[jnp.where(places < fixed, places, passed)]].set(jnp.asarray(tallies, jnp.int32))

    tallies = jnp.where(number % 4 == 0, named(heavy_load, number // 4), named(common, number - number // 4 - 1))
    mixed = jax.random.permutation(jax.random.fold_in(own, 3), amount)
    donor, sink = mixed[0:amount // 2 * 2:2], mixed[1:amount // 2 * 2:2]
    slack = jnp.minimum(tallies[donor] - 1, reach - tallies[sink]) // 2
    slack = jnp.where((donor == ranking[0]) | (sink == ranking[0]) | (tallies[sink] == 0), 0, jnp.maximum(slack, 0))
    passed = jax.random.randint(jax.random.fold_in(own, 4), (amount // 2,), 0, 1 << 20) % (slack + 1)
    tallies = tallies.at[donor].add(-passed).at[sink].add(passed)
    members = jnp.searchsorted(jnp.cumsum(tallies), jnp.arange(rows * top), side="right").astype(jnp.int32)
    grid = members.reshape(top, rows).T
    grid = grid[jax.random.permutation(jax.random.fold_in(own, 1), rows)]
    offset_by = jax.random.randint(jax.random.fold_in(own, 2), (rows, 1), 0, top)
    return jnp.take_along_axis(grid, (jnp.arange(top)[None, :] + offset_by) % top, axis=1)


def load_shares(number_of, total, bound, skew, full):
    loads = [(1 << 20) // math.isqrt(rank ** skew) + 1 for rank in range(1, number_of + 1)]
    largest = bound if full else min(bound, max(-(-total // number_of), total * loads[0] // sum(loads)))
    least = 1 if total - largest >= number_of - 1 else 0
    holding, surplus = [largest] + [least] * (number_of - 1), total - largest - least * (number_of - 1)
    while surplus > 0:
        free = [i for i in range(1, number_of) if holding[i] < largest] or [i for i in range(1, number_of) if holding[i] < bound]
        pool, left = sum([loads[i] for i in free]), surplus
        for i in free:
            extra = min(bound - holding[i], max(1, left * loads[i] // pool), surplus)
            holding[i] = holding[i] + extra
            surplus = surplus - extra
    return np.array(holding)


def scatter_about(rng, shape, width, most, split=(), kind=jnp.bfloat16):
    gain = steps_of(rng, shape, split, -0.22, 0.18) if split else 1.0
    drawn = jax.random.normal(rng, shape, jnp.float32) * width * gain
    return jnp.minimum(jnp.maximum(drawn, -most), most).astype(kind)


def setup_inputs(seed: int = 0) -> dict:
    keys = jax.random.split(jax.random.key(seed), 12)
    right_side = scatter_about(keys[0], (P_SIZE, NODES), 1.0, 6.0, ((0, 4), (1, 64)), jnp.float32)
    diag_blocks = draw_diag_blocks(jax.random.fold_in(keys[11], 71), 0)
    off_blocks = scatter_about(keys[2], (NB_TOTAL, KB, 4096), 0.2, 3.0, ((0, 64),), jnp.float32)
    smoother = draw_smoother(jax.random.fold_in(keys[11], 71), 0)
    col_index = plant(jax.random.randint(keys[4], (NB_TOTAL, KB), 0, NB_DEV + 2 * H), jax.random.fold_in(keys[4], 1), 0, (NB_DEV + 2 * H) - 1).astype(jnp.int32)
    send_list = plant(jax.random.randint(keys[5], (NB_TOTAL * 2 * H // NB_DEV,), 0, NB_DEV), jax.random.fold_in(keys[5], 1), 0, NB_DEV - 1).astype(jnp.int32)
    agg_map = plant(jax.random.randint(keys[6], (NODES,), 0, NA_DEV), jax.random.fold_in(keys[6], 1), 0, NA_DEV - 1).astype(jnp.int32)
    owner_map_keys = jax.random.split(jax.random.fold_in(keys[7], 1), NA_TOTAL // NA_DEV)
    owner_map_turns = jax.random.permutation(jax.random.fold_in(keys[7], 3), NA_TOTAL // NA_DEV)
    owner_map = jax.vmap(lambda own, number: shared_out(jax.random.fold_in(keys[7], 2), own, number, NA_DEV, NOWN, 1, CAP, 2))(owner_map_keys, owner_map_turns).reshape((NA_TOTAL, 1))
    coarse_diag = jnp.clip(jnp.exp(math.log(4.0) - 1.3862944 * jax.random.uniform(keys[8], (NA_TOTAL,), jnp.float32) ** steps_of(keys[8], (NA_TOTAL,), ((0, 64),), -0.2, 0.2)), 1.0, 4.0)
    coarse_weight = jnp.clip(jnp.exp(math.log(0.001953125) - 2.3025851 * jax.random.uniform(keys[9], (NA_TOTAL,), jnp.float32) ** steps_of(keys[9], (NA_TOTAL,), ((0, 64),), -0.2, 0.2)), 0.0001953125, 0.001953125)
    coarse_gain = jnp.clip(jnp.exp(math.log(2.0) - 2.3025851 * jax.random.uniform(keys[10], (NA_TOTAL,), jnp.float32) ** steps_of(keys[10], (NA_TOTAL,), ((0, 64),), -0.2, 0.2)), 0.2, 2.0)
    return dict(right_side=right_side, diag_blocks=diag_blocks, off_blocks=off_blocks, smoother=smoother, col_index=col_index, send_list=send_list, agg_map=agg_map, owner_map=owner_map, coarse_diag=coarse_diag, coarse_weight=coarse_weight, coarse_gain=coarse_gain)


def global_columns(col_index, send_list):
    dev = (jnp.arange(NB_TOTAL) // NB_DEV).astype(jnp.int32)
    sends = send_list.reshape(N_NODES, 2 * H)
    before = ((dev - 1) % N_NODES)[:, None]
    after = ((dev + 1) % N_NODES)[:, None]
    own_col = dev[:, None] * NB_DEV + col_index
    prev_pos = jnp.clip(col_index - NB_DEV, 0, H - 1)
    next_pos = jnp.clip(col_index - NB_DEV - H, 0, H - 1)
    from_prev = before * NB_DEV + sends[before, H + prev_pos]
    from_next = after * NB_DEV + sends[after, next_pos]
    return jnp.where(col_index < NB_DEV, own_col, jnp.where(col_index < NB_DEV + H, from_prev, from_next)).astype(jnp.int32)

def reference(right_side, diag_blocks, off_blocks, smoother, col_index, send_list, agg_map, owner_map, coarse_diag, coarse_weight, coarse_gain):
    hi = lax.Precision.HIGHEST
    gcol = global_columns(col_index, send_list)
    diag_mats = diag_blocks.reshape(NB_TOTAL, 64, 64)
    off_mats = off_blocks.reshape(NB_TOTAL, KB, 64, 64)
    smooth_mats = smoother.reshape(NB_TOTAL, 64, 64)

    def apply_op(field):

        def one_term(vec):
            blocks = vec.reshape(NB_TOTAL, 64)
            own = jnp.einsum('bij,bj->bi', diag_mats, blocks, precision=hi)
            far = jnp.einsum('bkij,bkj->bi', off_mats, blocks[gcol], precision=hi)
            return (own + far).reshape(-1)
        return lax.map(one_term, field)

    def smooth(field):

        def one_term(vec):
            return jnp.einsum('bij,bj->bi', smooth_mats, vec.reshape(NB_TOTAL, 64), precision=hi).reshape(-1)
        return lax.map(one_term, field)
    first = smooth(right_side)
    second = first + smooth(right_side - apply_op(first))
    resid = right_side - apply_op(second)
    gagg = (jnp.arange(NODES) // (NB_DEV * 64) * NA_DEV + agg_map).astype(jnp.int32)
    coarse_res = jax.ops.segment_sum(resid.T, gagg, num_segments=NA_TOTAL).T
    owner = owner_map[:, 0]
    corr = coarse_res / coarse_diag
    for sweep in range(CSWEEPS - 1):
        sums = jax.ops.segment_sum((coarse_weight * corr).T, owner, num_segments=NOWN).T
        corr = corr + (coarse_res - coarse_diag * corr + coarse_gain * sums[:, owner]) / coarse_diag
    third = second + corr[:, gagg]
    solution_field = third + smooth(right_side - apply_op(third))
    final = right_side - apply_op(solution_field)
    ratio = jnp.sqrt(jnp.sum(final * final) / (jnp.sum(right_side * right_side) + 1e-06))
    return (solution_field, ratio)
```

```python
import functools

import jax
import jax.numpy as jnp
from jax import lax
from jax.experimental import pallas as pl
from jax.experimental.pallas import tpu as pltpu
from jax.sharding import PartitionSpec as P

NB = 64
H = 8
KB = 4
NA = 256
NOWN = 16
TERMS = 30
R = 32
R1 = R + NOWN
TILES = NB // 2
UN = 4
YC = 8
YS = 4
CS = 2
MESH = pl.DeviceIdType.MESH
F32 = jnp.float32
BF16 = jnp.bfloat16


def dot_nt(a, b, precision=None):
    return lax.dot_general(
        a, b, (((1,), (1,)), ((), ())), precision=precision, preferred_element_type=F32
    )


def dot_nn(a, b):
    return lax.dot_general(a, b, (((1,), (0,)), ((), ())), preferred_element_type=F32)


def split(v):
    hi = v.astype(BF16)
    return hi, (v - hi.astype(F32)).astype(BF16)


def swap(v):
    return pltpu.roll(v, 64, 1)


def kernel(
    zs,
    xs,
    col,
    send_list,
    rhs_hbm,
    diag_hbm,
    off_hbm,
    smooth_hbm,
    agg_hbm,
    owner_hbm,
    cdiag_hbm,
    cweight_hbm,
    cgain_hbm,
    out_hbm,
    ratio_ref,
    rhs_v,
    diag_v,
    off_v,
    smooth_v,
    agg_v,
    owner_v,
    cdiag_v,
    cweight_v,
    cgain_v,
    mats,
    fields,
    hot,
    b_f,
    x_f,
    r_f,
    w_f,
    c_x,
    c_r,
    tmp,
    sol_v,
    snd1,
    rcv1,
    snd2,
    rcv2,
    sum_a,
    sum_b,
    norm_a,
    norm_b,
    load_sem,
    halo_send,
    halo_recv,
    a_send,
    a_recv,
    b_send,
    b_recv,
    na_send,
    na_recv,
    nb_send,
    nb_recv,
):
    n = lax.axis_index("nodes")
    x = lax.axis_index("chaos")
    count = zs * YC
    z = n // YC
    yc = n % YC
    y = yc // CS
    c = yc % CS
    right = lax.rem(n + 1, count)
    left = lax.rem(n + count - 1, count)

    def node(zz, yy, cc):
        return (zz * YS + yy) * CS + cc

    loads = [
        pltpu.make_async_copy(src, dst, load_sem.at[i])
        for i, (src, dst) in enumerate(
            [
                (agg_hbm, agg_v),
                (owner_hbm, owner_v),
                (cdiag_hbm, cdiag_v),
                (cweight_hbm, cweight_v),
                (cgain_hbm, cgain_v),
                (smooth_hbm, smooth_v),
                (diag_hbm, diag_v),
                (rhs_hbm, rhs_v),
                (off_hbm, off_v),
            ]
        )
    ]
    for load in loads:
        load.start()

    peers_a = [(z * YC + lax.rem(yc + j, YC), x) for j in range(1, YC)]
    peers_b = [(lax.rem(z + j, zs) * YC + yc, x) for j in range(1, zs)]
    peers_na = [
        (node(z, lax.rem(y + j % YS, YS), c), lax.rem(x + j // YS, xs))
        for j in range(1, xs * YS)
    ]
    peers_nb = [
        (node(lax.rem(z + j // CS, zs), y, lax.rem(c + j % CS, CS)), x)
        for j in range(1, zs * CS)
    ]
    barrier = pltpu.get_barrier_semaphore()
    greeted = [(left, x), (right, x)] + peers_a + peers_b + peers_na + peers_nb
    for peer in greeted:
        pl.semaphore_signal(barrier, inc=1, device_id=peer, device_id_type=MESH)

    lane = lax.broadcasted_iota(jnp.int32, (1, 128), 1)
    low = lane < 64
    keep_low = low.astype(F32).astype(BF16)
    keep_high = (lane >= 64).astype(F32).astype(BF16)

    def pick(a, b):
        return jnp.where(low, a, b)

    def combine(out, rows):
        u = out[:rows]
        w = u + jnp.where(low, out[rows:], 0.0)
        return w + swap(w)

    def put(slot, blk, both, rows):
        hi, lo = split(both)
        fields[slot, blk, 0, 0:rows, :] = hi * keep_low
        fields[slot, blk, 0, rows : 2 * rows, :] = lo * keep_low
        fields[slot, blk, 1, 0:rows, :] = hi * keep_high
        fields[slot, blk, 1, rows : 2 * rows, :] = lo * keep_high

    def apply_a(slot, blk, rows):
        cols = [col[k, blk] for k in range(KB)]
        near = [
            fields[slot, cols[k], 0, 0 : 2 * rows, :] + fields[slot, cols[k + 1], 1, 0 : 2 * rows, :]
            for k in (0, 2)
        ]
        own = fields[slot, blk, 0, 0 : 2 * rows, :]
        lhs = jnp.concatenate(near + [own], axis=1)
        return combine(dot_nt(lhs, mats[blk]), rows)

    def apply_s(both, blk, rows):
        hi, lo = split(both)
        lhs = jnp.concatenate([hi * keep_high, lo * keep_high], axis=0)
        return combine(dot_nt(lhs, mats[blk, :, 256:384]), rows)

    def halo_copies(stage, snd, rcv, slot):
        return [
            pltpu.make_async_remote_copy(
                src_ref=snd.at[slot, side],
                dst_ref=rcv.at[slot, side],
                send_sem=halo_send.at[stage, side],
                recv_sem=halo_recv.at[stage, side],
                device_id=(left if side == 0 else right, x),
                device_id_type=MESH,
            )
            for side in (0, 1)
        ]

    def take_halo(copies, rcv, rslot, slot, rows):
        for side, base in ((1, NB), (0, NB + H)):
            copies[side].wait_recv()
            for m in range(H // 2):
                tile = rcv[rslot, side, m]
                other = swap(tile)
                put(slot, base + 2 * m, pick(tile, other), rows)
                put(slot, base + 2 * m + 1, pick(other, tile), rows)

    def export_from(ref, snd, slot):
        for side in (0, 1):
            for m in range(H // 2):
                first = send_list[side * H + 2 * m]
                second = send_list[side * H + 2 * m + 1]
                snd[slot, side, m] = pick(ref[first], ref[second])

    def loop(body, steps, unroll):
        def step(i, carry):
            body([i * unroll + j for j in range(unroll)])
            return carry

        lax.fori_loop(0, steps // unroll, step, 0)

    for load in loads[:5]:
        load.wait()
    inv = 1.0 / cdiag_v[...]
    gain = cgain_v[...] * inv
    weight = cweight_v[...]
    own_hot = (
        lax.broadcasted_iota(jnp.int32, (NOWN, NA), 0) == owner_v[...]
    ).astype(F32)
    rows_a = lax.broadcasted_iota(jnp.int32, (NA, 128), 0)

    def build_hot(ts):
        for t in ts:
            hot[t] = (rows_a == agg_v[pl.ds(t, 1), :]).astype(F32).astype(BF16)

    loop(build_hot, TILES, 2)

    g_hi, g_lo = split(own_hot * gain)
    g_lhs = jnp.concatenate([g_hi, g_lo], axis=0)

    def build_pg(ts):
        for t in ts:
            both = dot_nn(g_lhs, hot[t])
            tile = both[:NOWN] + both[NOWN:]
            other = swap(tile)
            x_f[2 * t, R:R1, :] = pick(tile, other)
            x_f[2 * t + 1, R:R1, :] = pick(other, tile)

    loop(build_pg, TILES, 4)

    def interleave(j, first, second):
        a, b = swap(first), swap(second)
        tmp[j, pl.ds(0, 32, stride=2), :] = pick(first, b)
        tmp[j, pl.ds(1, 32, stride=2), :] = pick(a, second)

    def settle(j, blk, at):
        hi, lo = split(tmp[j])
        mats[blk, 0:64, at : at + 128] = hi
        mats[blk, 64:128, at : at + 128] = lo

    def strided8(ref, blk):
        return ref[pl.ds((blk // 8) * 256 + blk % 8, 32, stride=8), :]

    for load in loads[5:8]:
        load.wait()

    def prep_own(bs):
        for j, blk in enumerate(bs):
            interleave(j, strided8(diag_v, blk), strided8(smooth_v, blk))
        for j, blk in enumerate(bs):
            settle(j, blk, 256)

    loop(prep_own, NB, UN)

    zero2 = jnp.zeros((2, 128), F32)

    def first_smooth(ts):
        for t in ts:
            tile = rhs_v[:, pl.ds(pl.multiple_of(t * 128, 128), 128)]
            tile = jnp.concatenate([tile, zero2], axis=0)
            other = swap(tile)
            for blk, both in ((2 * t, pick(tile, other)), (2 * t + 1, pick(other, tile))):
                b_f[blk] = both
                x_f[blk, 0:R, :] = apply_s(both, blk, R)
                put(0, blk, x_f[blk], R1)

    loop(first_smooth, TILES, 2)

    pl.semaphore_wait(barrier, len(greeted))
    export_from(x_f, snd1, 0)
    halo1 = halo_copies(0, snd1, rcv1, 0)
    for copy in halo1:
        copy.start()

    loads[8].wait()

    def prep_off(bs):
        for j, blk in enumerate(bs):
            parts = [off_v[pl.ds(blk * 128 + k, 32, stride=4), :] for k in range(KB)]
            interleave(2 * j, parts[0], parts[1])
            interleave(2 * j + 1, parts[2], parts[3])
        for j, blk in enumerate(bs):
            settle(2 * j, blk, 0)
            settle(2 * j + 1, blk, 128)

    loop(prep_off, NB, UN)

    none = jnp.zeros((NOWN, 128), F32)

    def second(blk):
        target = jnp.concatenate([b_f[blk], none], axis=0)
        resid = target - apply_a(0, blk, R1)
        return x_f[blk] + apply_s(resid, blk, R1)

    take_halo(halo1, rcv1, 0, 0, R1)

    def second_export(ms):
        done = [second(send_list[m]) for m in ms]
        for i in range(0, len(ms), 2):
            e_tile = pick(done[i], done[i + 1])
            snd1[1, ms[i] // H, (ms[i] % H) // 2] = e_tile

    loop(second_export, 2 * H, UN)
    halo2 = halo_copies(1, snd1, rcv1, 1)
    for copy in halo2:
        copy.start()

    def second_all(bs):
        done = [second(blk) for blk in bs]
        for blk, both in zip(bs, done):
            put(1, blk, both, R1)
            w_f[blk] = both

    loop(second_all, NB, UN)
    take_halo(halo2, rcv1, 1, 1, R1)

    def triple(tile):
        hi, lo = split(tile)
        return jnp.concatenate([hi, hi, lo], axis=0)

    def resid_all(bs):
        out = []
        for blk in bs:
            target = jnp.concatenate([b_f[blk], none], axis=0)
            out.append(target - apply_a(1, blk, R1))
        for i in range(0, len(bs), 2):
            t = bs[i] // 2
            tile = pick(out[i], out[i + 1])
            r_f[bs[i]] = out[i][:R]
            r_f[bs[i + 1]] = out[i + 1][:R]
            c_r[t] = triple(tile[R:])
            c_x[t] = triple(pick(w_f[bs[i], R:R1, :], w_f[bs[i + 1], R:R1, :]))

    loop(resid_all, NB, UN)

    def restrict(i, acc):
        for j in range(2):
            t = i * 2 + j
            hi, lo = split(pick(r_f[2 * t], r_f[2 * t + 1]))
            acc = acc + dot_nt(jnp.concatenate([hi, lo], axis=0), hot[t])
        return acc

    acc = lax.fori_loop(0, TILES // 2, restrict, jnp.zeros((2 * R, NA), F32))
    coarse = (acc[:R] + acc[R:]) * inv
    row = lax.broadcasted_iota(jnp.int32, (R, NA), 0)
    weighted = jnp.where(row == TERMS, gain, coarse) * weight
    part = dot_nt(own_hot, weighted, lax.Precision.HIGHEST)
    sum_a[0] = jnp.concatenate([part, jnp.zeros((NOWN, 128 - R), F32)], axis=1)
    copies_a = [
        pltpu.make_async_remote_copy(
            src_ref=sum_a.at[0],
            dst_ref=sum_a.at[j + 1],
            send_sem=a_send.at[j],
            recv_sem=a_recv.at[j],
            device_id=peer,
            device_id_type=MESH,
        )
        for j, peer in enumerate(peers_a)
    ]
    for copy in copies_a:
        copy.start()

    e_hi, e_lo = split(coarse)
    e_lhs = jnp.concatenate([e_hi, e_lo], axis=0)

    def prolong(ts):
        for t in ts:
            both = dot_nn(e_lhs, hot[t])
            tile = both[:R] + both[R:]
            other = swap(tile)
            for blk, dup in ((2 * t, pick(tile, other)), (2 * t + 1, pick(other, tile))):
                b_f[blk] = dup
                put(0, blk, dup, R)

    loop(prolong, TILES, 4)
    export_from(b_f, snd2, 0)
    halo3 = halo_copies(2, snd2, rcv2, 0)
    for copy in halo3:
        copy.start()
    for copy in copies_a:
        copy.wait_recv()
    sum_b[0] = jnp.sum(sum_a[...], axis=0)
    copies_b = [
        pltpu.make_async_remote_copy(
            src_ref=sum_b.at[0],
            dst_ref=sum_b.at[j + 1],
            send_sem=b_send.at[j],
            recv_sem=b_recv.at[j],
            device_id=peer,
            device_id_type=MESH,
        )
        for j, peer in enumerate(peers_b)
    ]
    for copy in copies_b:
        copy.start()
    take_halo(halo3, rcv2, 0, 0, R)

    def third(blk):
        resid = r_f[blk] - apply_a(0, blk, R)
        return resid, apply_s(resid, blk, R)

    def third_export(ms):
        done = [third(send_list[m])[1] for m in ms]
        for i in range(0, len(ms), 2):
            snd2[1, ms[i] // H, (ms[i] % H) // 2] = pick(done[i], done[i + 1])

    loop(third_export, 2 * H, UN)
    halo4 = halo_copies(3, snd2, rcv2, 1)
    for copy in halo4:
        copy.start()

    def third_all(bs):
        done = [third(blk) for blk in bs]
        for blk, (resid, step) in zip(bs, done):
            put(1, blk, step, R)
            x_f[blk, 0:R, :] = resid
            b_f[blk] = b_f[blk] + step + w_f[blk, 0:R, :]

    loop(third_all, NB, UN)

    for copy in copies_b:
        copy.wait_recv()
    total = jnp.sum(sum_b[...], axis=0)[:, 0:R]
    total = total * (1.0 + total[:, TERMS : TERMS + 1])
    keep = lax.broadcasted_iota(jnp.int32, (NOWN, R), 1) < TERMS
    s_hi, s_lo = split(jnp.where(keep, total, 0.0).T)
    s_lhs = jnp.concatenate([s_hi, s_lo, s_hi], axis=1)

    def finish(ts):
        for t in ts:
            tile = pick(b_f[2 * t], b_f[2 * t + 1]) + dot_nn(s_lhs, c_x[t])
            sol_v[:, pl.ds(pl.multiple_of(t * 128, 128), 128)] = tile[:TERMS]

    loop(finish, TILES, 4)
    store = pltpu.make_async_copy(sol_v, out_hbm, load_sem.at[0])
    store.start()

    take_halo(halo4, rcv2, 1, 1, R)

    def final(i, acc):
        for j in range(2):
            t = i * 2 + j
            parts = [x_f[blk, 0:R, :] - apply_a(1, blk, R) for blk in (2 * t, 2 * t + 1)]
            tile = pick(parts[0], parts[1]) + dot_nn(s_lhs, c_r[t])
            acc = acc + tile * tile
        return acc

    acc = lax.fori_loop(0, TILES // 2, final, jnp.zeros((R, 128), F32))

    def right_norm(i, acc):
        tile = rhs_v[:, pl.ds(pl.multiple_of(i * 128, 128), 128)]
        return acc + tile * tile

    acc_b = lax.fori_loop(0, TILES, right_norm, jnp.zeros((TERMS, 128), F32))
    line = lax.broadcasted_iota(jnp.int32, (8, 128), 0)
    norm_a[0] = jnp.where(
        line == 0,
        jnp.sum(acc, axis=0, keepdims=True),
        jnp.where(line == 1, jnp.sum(acc_b, axis=0, keepdims=True), 0.0),
    )
    copies_na = [
        pltpu.make_async_remote_copy(
            src_ref=norm_a.at[0],
            dst_ref=norm_a.at[j + 1],
            send_sem=na_send.at[j],
            recv_sem=na_recv.at[j],
            device_id=peer,
            device_id_type=MESH,
        )
        for j, peer in enumerate(peers_na)
    ]
    for copy in copies_na:
        copy.start()
    for copy in copies_na:
        copy.wait_recv()
    norm_b[0] = jnp.sum(norm_a[...], axis=0)
    copies_nb = [
        pltpu.make_async_remote_copy(
            src_ref=norm_b.at[0],
            dst_ref=norm_b.at[j + 1],
            send_sem=nb_send.at[j],
            recv_sem=nb_recv.at[j],
            device_id=peer,
            device_id_type=MESH,
        )
        for j, peer in enumerate(peers_nb)
    ]
    for copy in copies_nb:
        copy.start()
    for copy in copies_nb:
        copy.wait_recv()
    sums = jnp.sum(jnp.sum(norm_b[...], axis=0), axis=1, keepdims=True)
    ratio_ref[...] = jnp.sqrt(sums[0:1] / (sums[1:2] + 1e-6))

    for copies in (halo1, halo2, halo3, halo4, copies_a, copies_b, copies_na, copies_nb):
        for copy in copies:
            copy.wait_send()
    store.wait()


def on_device(
    zs,
    xs,
    right_side,
    diag_blocks,
    off_blocks,
    smoother,
    col_index,
    send_list,
    agg_map,
    owner_map,
    coarse_diag,
    coarse_weight,
    coarse_gain,
):
    def rows_of(v):
        return v.reshape(8, 8, 32, 128).transpose(0, 2, 1, 3).reshape(NB * 32, 128)

    off = off_blocks.reshape(NB, KB, 32, 128).transpose(0, 2, 1, 3).reshape(NB * KB * 32, 128)
    hbm = pl.BlockSpec(memory_space=pl.ANY)
    smem = pl.BlockSpec(memory_space=pltpu.SMEM)
    dma = pltpu.SemaphoreType.DMA
    scratch = [
        pltpu.VMEM((TERMS, NB * 64), F32),
        pltpu.VMEM((NB * 32, 128), F32),
        pltpu.VMEM((NB * KB * 32, 128), F32),
        pltpu.VMEM((NB * 32, 128), F32),
        pltpu.VMEM((TILES, 128), jnp.int32),
        pltpu.VMEM((1, NA), jnp.int32),
        pltpu.VMEM((1, NA), F32),
        pltpu.VMEM((1, NA), F32),
        pltpu.VMEM((1, NA), F32),
        pltpu.VMEM((NB, 128, 384), BF16),
        pltpu.VMEM((2, NB + 2 * H, 2, 2 * R1, 128), BF16),
        pltpu.VMEM((TILES, NA, 128), BF16),
        pltpu.VMEM((NB, R, 128), F32),
        pltpu.VMEM((NB, R1, 128), F32),
        pltpu.VMEM((NB, R, 128), F32),
        pltpu.VMEM((NB, R1, 128), F32),
        pltpu.VMEM((TILES, 3 * NOWN, 128), BF16),
        pltpu.VMEM((TILES, 3 * NOWN, 128), BF16),
        pltpu.VMEM((2 * UN, 64, 128), F32),
        pltpu.VMEM((TERMS, NB * 64), F32),
        pltpu.VMEM((2, 2, H // 2, R1, 128), F32),
        pltpu.VMEM((2, 2, H // 2, R1, 128), F32),
        pltpu.VMEM((2, 2, H // 2, R, 128), F32),
        pltpu.VMEM((2, 2, H // 2, R, 128), F32),
        pltpu.VMEM((YC, NOWN, 128), F32),
        pltpu.VMEM((zs, NOWN, 128), F32),
        pltpu.VMEM((xs * YS, 8, 128), F32),
        pltpu.VMEM((zs * CS, 8, 128), F32),
        dma((9,)),
        dma((4, 2)),
        dma((4, 2)),
        dma((YC,)),
        dma((YC,)),
        dma((zs,)),
        dma((zs,)),
        dma((xs * YS,)),
        dma((xs * YS,)),
        dma((zs * CS,)),
        dma((zs * CS,)),
    ]
    out, ratio = pl.pallas_call(
        functools.partial(kernel, zs, xs),
        out_shape=(
            jax.ShapeDtypeStruct((TERMS, NB * 64), F32),
            jax.ShapeDtypeStruct((1, 1), F32),
        ),
        in_specs=[smem, smem] + [hbm] * 9,
        out_specs=(hbm, pl.BlockSpec(memory_space=pltpu.VMEM)),
        scratch_shapes=scratch,
        compiler_params=pltpu.CompilerParams(
            collective_id=0, has_side_effects=True, vmem_limit_bytes=56 * 1024 * 1024
        ),
    )(
        col_index.T,
        send_list,
        right_side,
        rows_of(diag_blocks),
        off,
        rows_of(smoother),
        agg_map.reshape(TILES, 128),
        owner_map.reshape(1, NA),
        coarse_diag.reshape(1, NA),
        coarse_weight.reshape(1, NA),
        coarse_gain.reshape(1, NA),
    )
    return out, ratio.reshape(())


def solution(mesh):
    placed = (
        P("chaos", "nodes"),
        P("nodes", None),
        P("nodes", None, None),
        P("nodes", None),
        P("nodes", None),
        P("nodes"),
        P("nodes"),
        P("nodes", None),
        P("nodes"),
        P("nodes"),
        P("nodes"),
    )
    return jax.shard_map(
        functools.partial(on_device, mesh.shape["nodes"] // YC, mesh.shape["chaos"]),
        mesh=mesh,
        in_specs=placed,
        out_specs=(P("chaos", "nodes"), P()),
        check_vma=False,
    )
```

```python
import functools
import itertools

import jax
import jax.numpy as jnp
from jax import lax
from jax.experimental import pallas as pl
from jax.experimental.pallas import tpu as pltpu
from jax.sharding import PartitionSpec as P

NB = 64
H = 8
KB = 4
NA = 256
NOWN = 16
TERMS = 30
R = 32
R1 = R + NOWN
TILES = NB // 2
UN = 32
YC = 8
YS = 4
CS = 2
MESH = pl.DeviceIdType.MESH
F32 = jnp.float32
BF16 = jnp.bfloat16


def dot_nt(a, b, precision=None):
    return lax.dot_general(
        a, b, (((1,), (1,)), ((), ())), precision=precision, preferred_element_type=F32
    )


def dot_nn(a, b):
    return lax.dot_general(a, b, (((1,), (0,)), ((), ())), preferred_element_type=F32)


def split(v):
    hi = v.astype(BF16)
    return hi, (v - hi.astype(F32)).astype(BF16)


def swap(v):
    return pltpu.roll(v, 64, 1)


def kernel(
    zs,
    xs,
    col,
    send_list,
    rhs_hbm,
    diag_hbm,
    off_hbm,
    smooth_hbm,
    agg_hbm,
    owner_hbm,
    cdiag_hbm,
    cweight_hbm,
    cgain_hbm,
    out_hbm,
    ratio_ref,
    rhs_v,
    diag_v,
    off_v,
    smooth_v,
    agg_v,
    owner_v,
    cdiag_v,
    cweight_v,
    cgain_v,
    mats,
    fields,
    hot,
    b_f,
    x_f,
    r_f,
    w_f,
    c_x,
    c_r,
    tmp,
    sol_v,
    snd1,
    rcv1,
    snd2,
    rcv2,
    sum_a,
    sum_b,
    norm_v,
    load_sem,
    halo_send,
    halo_recv,
    a_send,
    a_recv,
    b_send,
    b_recv,
    n_send,
    n_recv,
):
    n = lax.axis_index("nodes")
    x = lax.axis_index("chaos")
    count = zs * YC
    z = n // YC
    yc = n % YC
    y = yc // CS
    c = yc % CS
    right = lax.rem(n + 1, count)
    left = lax.rem(n + count - 1, count)

    def node(zz, yy, cc):
        return (zz * YS + yy) * CS + cc

    loads = [
        pltpu.make_async_copy(src, dst, load_sem.at[i])
        for i, (src, dst) in enumerate(
            [
                (agg_hbm, agg_v),
                (owner_hbm, owner_v),
                (cdiag_hbm, cdiag_v),
                (cweight_hbm, cweight_v),
                (cgain_hbm, cgain_v),
                (smooth_hbm, smooth_v),
                (diag_hbm, diag_v),
                (rhs_hbm, rhs_v),
                (off_hbm, off_v),
            ]
        )
    ]
    for load in loads:
        load.start()

    peers_a = [(z * YC + lax.rem(yc + j, YC), x) for j in range(1, YC)]
    peers_b = [(lax.rem(z + j, zs) * YC + yc, x) for j in range(1, zs)]
    dims = {"z": zs, "y": YS, "c": CS, "x": xs}
    at = {"z": z, "y": y, "c": c, "x": x}

    def group(axes):
        peers = []
        for offs in itertools.product(*[range(dims[a]) for a in axes]):
            if any(offs):
                to = dict(at)
                for a, o in zip(axes, offs):
                    if o:
                        to[a] = lax.rem(at[a] + o, dims[a])
                peers.append((node(to["z"], to["y"], to["c"]), to["x"]))
        return peers

    norm_groups = [group(axes) for axes in ['xy', 'zc']]
    barrier = pltpu.get_barrier_semaphore()
    greeted = [(left, x), (right, x)] + peers_a + peers_b + sum(norm_groups, [])
    for peer in greeted:
        pl.semaphore_signal(barrier, inc=1, device_id=peer, device_id_type=MESH)

    lane = lax.broadcasted_iota(jnp.int32, (1, 128), 1)
    low = lane < 64
    keep_low = low.astype(F32).astype(BF16)
    keep_high = (lane >= 64).astype(F32).astype(BF16)

    def pick(a, b):
        return jnp.where(low, a, b)

    def combine(out, rows):
        u = out[:rows]
        w = u + jnp.where(low, out[rows:], 0.0)
        return w + swap(w)

    def put(slot, blk, both, rows):
        hi, lo = split(both)
        fields[slot, blk, 0, 0:rows, :] = hi * keep_low
        fields[slot, blk, 0, rows : 2 * rows, :] = lo * keep_low
        fields[slot, blk, 1, 0:rows, :] = hi * keep_high
        fields[slot, blk, 1, rows : 2 * rows, :] = lo * keep_high

    def apply_a(slot, blk, rows):
        cols = [col[k, blk] for k in range(KB)]
        near = [
            fields[slot, cols[k], 0, 0 : 2 * rows, :] + fields[slot, cols[k + 1], 1, 0 : 2 * rows, :]
            for k in (0, 2)
        ]
        own = fields[slot, blk, 0, 0 : 2 * rows, :]
        lhs = jnp.concatenate(near + [own], axis=1)
        return combine(dot_nn(lhs, mats[blk]), rows)

    def apply_s(both, blk, rows):
        hi, lo = split(both)
        lhs = jnp.concatenate([hi * keep_high, lo * keep_high], axis=0)
        return combine(dot_nn(lhs, mats[blk, 256:384, :]), rows)

    def halo_copies(stage, snd, rcv, slot):
        return [
            pltpu.make_async_remote_copy(
                src_ref=snd.at[slot, side],
                dst_ref=rcv.at[slot, side],
                send_sem=halo_send.at[stage, side],
                recv_sem=halo_recv.at[stage, side],
                device_id=(left if side == 0 else right, x),
                device_id_type=MESH,
            )
            for side in (0, 1)
        ]

    def take_halo(copies, rcv, rslot, slot, rows):
        for side, base in ((1, NB), (0, NB + H)):
            copies[side].wait_recv()
            for m in range(H // 2):
                tile = rcv[rslot, side, m]
                other = swap(tile)
                put(slot, base + 2 * m, pick(tile, other), rows)
                put(slot, base + 2 * m + 1, pick(other, tile), rows)

    def export_from(ref, snd, slot):
        for side in (0, 1):
            for m in range(H // 2):
                first = send_list[side * H + 2 * m]
                second = send_list[side * H + 2 * m + 1]
                snd[slot, side, m] = pick(ref[first], ref[second])

    def loop(body, steps, unroll):
        def step(i, carry):
            body([i * unroll + j for j in range(unroll)])
            return carry

        lax.fori_loop(0, steps // unroll, step, 0)

    for load in loads[:5]:
        load.wait()
    inv = 1.0 / cdiag_v[...]
    gain = cgain_v[...] * inv
    weight = cweight_v[...]
    own_hot = (
        lax.broadcasted_iota(jnp.int32, (NOWN, NA), 0) == owner_v[...]
    ).astype(F32)
    rows_a = lax.broadcasted_iota(jnp.int32, (NA, 128), 0)

    def build_hot(ts):
        for t in ts:
            hot[t] = (rows_a == agg_v[pl.ds(t, 1), :]).astype(F32).astype(BF16)

    loop(build_hot, TILES, 4)

    g_hi, g_lo = split(own_hot * gain)
    g_lhs = jnp.concatenate([g_hi, g_lo], axis=0)

    def build_pg(ts):
        for t in ts:
            both = dot_nn(g_lhs, hot[t])
            tile = both[:NOWN] + both[NOWN:]
            other = swap(tile)
            x_f[2 * t, R:R1, :] = pick(tile, other)
            x_f[2 * t + 1, R:R1, :] = pick(other, tile)

    loop(build_pg, TILES, 8)

    def interleave(j, first, second):
        a, b = swap(first), swap(second)
        tmp[j, pl.ds(0, 32, stride=2), :] = pick(first, b)
        tmp[j, pl.ds(1, 32, stride=2), :] = pick(a, second)

    def settle(j, blk, at):
        hi, lo = split(tmp[j])
        mats[blk, at : at + 128, :] = jnp.concatenate([hi, lo], axis=0).T

    def strided8(ref, blk):
        return ref[pl.ds((blk // 8) * 256 + blk % 8, 32, stride=8), :]

    for load in loads[5:8]:
        load.wait()

    def prep_own(bs):
        for j, blk in enumerate(bs):
            interleave(j, strided8(diag_v, blk), strided8(smooth_v, blk))
        for j, blk in enumerate(bs):
            settle(j, blk, 256)

    loop(prep_own, NB, UN)

    zero2 = jnp.zeros((2, 128), F32)

    def first_smooth(ts):
        for t in ts:
            tile = rhs_v[:, pl.ds(pl.multiple_of(t * 128, 128), 128)]
            tile = jnp.concatenate([tile, zero2], axis=0)
            other = swap(tile)
            for blk, both in ((2 * t, pick(tile, other)), (2 * t + 1, pick(other, tile))):
                b_f[blk] = both
                x_f[blk, 0:R, :] = apply_s(both, blk, R)
                put(0, blk, x_f[blk], R1)

    loop(first_smooth, TILES, 16)

    pl.semaphore_wait(barrier, len(greeted))
    export_from(x_f, snd1, 0)
    halo1 = halo_copies(0, snd1, rcv1, 0)
    for copy in halo1:
        copy.start()

    loads[8].wait()

    def prep_off(bs):
        for j, blk in enumerate(bs):
            parts = [off_v[pl.ds(blk * 128 + k, 32, stride=4), :] for k in range(KB)]
            interleave(2 * j, parts[0], parts[1])
            interleave(2 * j + 1, parts[2], parts[3])
        for j, blk in enumerate(bs):
            settle(2 * j, blk, 0)
            settle(2 * j + 1, blk, 128)

    loop(prep_off, NB, UN)

    none = jnp.zeros((NOWN, 128), F32)

    def second(blk):
        target = jnp.concatenate([b_f[blk], none], axis=0)
        resid = target - apply_a(0, blk, R1)
        return x_f[blk] + apply_s(resid, blk, R1)

    take_halo(halo1, rcv1, 0, 0, R1)

    def second_a(bs):
        out = []
        for blk in bs:
            target = jnp.concatenate([b_f[blk], none], axis=0)
            out.append(target - apply_a(0, blk, R1))
        for blk, r in zip(bs, out):
            w_f[blk] = r

    loop(second_a, NB, UN)

    def second_all(bs):
        done = [x_f[blk] + apply_s(w_f[blk], blk, R1) for blk in bs]
        for blk, both in zip(bs, done):
            put(1, blk, both, R1)
            w_f[blk] = both

    loop(second_all, NB, UN)
    export_from(w_f, snd1, 1)
    halo2 = halo_copies(1, snd1, rcv1, 1)
    for copy in halo2:
        copy.start()

    take_halo(halo2, rcv1, 1, 1, R1)

    def triple(tile):
        hi, lo = split(tile)
        return jnp.concatenate([hi, hi, lo], axis=0)

    def resid_all(bs):
        out = []
        for blk in bs:
            target = jnp.concatenate([b_f[blk], none], axis=0)
            out.append(target - apply_a(1, blk, R1))
        for i in range(0, len(bs), 2):
            t = bs[i] // 2
            tile = pick(out[i], out[i + 1])
            r_f[bs[i]] = out[i][:R]
            r_f[bs[i + 1]] = out[i + 1][:R]
            c_r[t] = triple(tile[R:])
            c_x[t] = triple(pick(w_f[bs[i], R:R1, :], w_f[bs[i + 1], R:R1, :]))

    loop(resid_all, NB, UN)

    def restrict(i, acc):
        for j in range(16):
            t = i * 16 + j
            hi, lo = split(pick(r_f[2 * t], r_f[2 * t + 1]))
            acc = acc + dot_nt(jnp.concatenate([hi, lo], axis=0), hot[t])
        return acc

    acc = lax.fori_loop(0, TILES // 16, restrict, jnp.zeros((2 * R, NA), F32))
    coarse = (acc[:R] + acc[R:]) * inv
    row = lax.broadcasted_iota(jnp.int32, (R, NA), 0)
    weighted = jnp.where(row == TERMS, gain, coarse) * weight
    part = dot_nt(own_hot, weighted, lax.Precision.HIGHEST)
    sum_a[0] = jnp.concatenate([part, jnp.zeros((NOWN, 128 - R), F32)], axis=1)
    copies_a = [
        pltpu.make_async_remote_copy(
            src_ref=sum_a.at[0],
            dst_ref=sum_a.at[j + 1],
            send_sem=a_send.at[j],
            recv_sem=a_recv.at[j],
            device_id=peer,
            device_id_type=MESH,
        )
        for j, peer in enumerate(peers_a)
    ]
    for copy in copies_a:
        copy.start()

    e_hi, e_lo = split(coarse)
    e_lhs = jnp.concatenate([e_hi, e_lo], axis=0)

    def prolong(ts):
        for t in ts:
            both = dot_nn(e_lhs, hot[t])
            tile = both[:R] + both[R:]
            other = swap(tile)
            for blk, dup in ((2 * t, pick(tile, other)), (2 * t + 1, pick(other, tile))):
                b_f[blk] = dup
                put(0, blk, dup, R)

    loop(prolong, TILES, 8)
    export_from(b_f, snd2, 0)
    halo3 = halo_copies(2, snd2, rcv2, 0)
    for copy in halo3:
        copy.start()
    for copy in copies_a:
        copy.wait_recv()
    sum_b[0] = jnp.sum(sum_a[...], axis=0)
    copies_b = [
        pltpu.make_async_remote_copy(
            src_ref=sum_b.at[0],
            dst_ref=sum_b.at[j + 1],
            send_sem=b_send.at[j],
            recv_sem=b_recv.at[j],
            device_id=peer,
            device_id_type=MESH,
        )
        for j, peer in enumerate(peers_b)
    ]
    for copy in copies_b:
        copy.start()
    take_halo(halo3, rcv2, 0, 0, R)

    def third(blk):
        resid = r_f[blk] - apply_a(0, blk, R)
        return resid, apply_s(resid, blk, R)

    def third_a(bs):
        out = [r_f[blk] - apply_a(0, blk, R) for blk in bs]
        for blk, r in zip(bs, out):
            x_f[blk, 0:R, :] = r

    loop(third_a, NB, UN)

    def third_all(bs):
        done = [apply_s(x_f[blk, 0:R, :], blk, R) for blk in bs]
        for blk, step in zip(bs, done):
            put(1, blk, step, R)
            r_f[blk] = step

    loop(third_all, NB, UN)
    export_from(r_f, snd2, 1)
    halo4 = halo_copies(3, snd2, rcv2, 1)
    for copy in halo4:
        copy.start()

    for copy in copies_b:
        copy.wait_recv()
    total = jnp.sum(sum_b[...], axis=0)[:, 0:R]
    total = total * (1.0 + total[:, TERMS : TERMS + 1])
    keep = lax.broadcasted_iota(jnp.int32, (NOWN, R), 1) < TERMS
    s_hi, s_lo = split(jnp.where(keep, total, 0.0).T)
    s_lhs = jnp.concatenate([s_hi, s_lo, s_hi], axis=1)

    def finish(ts):
        for t in ts:
            parts = [b_f[blk] + r_f[blk] + w_f[blk, 0:R, :] for blk in (2 * t, 2 * t + 1)]
            tile = pick(parts[0], parts[1]) + dot_nn(s_lhs, c_x[t])
            sol_v[:, pl.ds(pl.multiple_of(t * 128, 128), 128)] = tile[:TERMS]

    loop(finish, TILES, 8)
    store = pltpu.make_async_copy(sol_v, out_hbm, load_sem.at[0])
    store.start()

    take_halo(halo4, rcv2, 1, 1, R)

    def final(i, acc):
        for j in range(16):
            t = i * 16 + j
            parts = [x_f[blk, 0:R, :] - apply_a(1, blk, R) for blk in (2 * t, 2 * t + 1)]
            tile = pick(parts[0], parts[1]) + dot_nn(s_lhs, c_r[t])
            acc = acc + tile * tile
        return acc

    acc = lax.fori_loop(0, TILES // 16, final, jnp.zeros((R, 128), F32))

    def right_norm(i, acc):
        tile = rhs_v[:, pl.ds(pl.multiple_of(i * 128, 128), 128)]
        return acc + tile * tile

    acc_b = lax.fori_loop(0, TILES, right_norm, jnp.zeros((TERMS, 128), F32))
    line = lax.broadcasted_iota(jnp.int32, (8, 128), 0)
    norm_v[0, 0] = jnp.where(
        line == 0,
        jnp.sum(acc, axis=0, keepdims=True),
        jnp.where(line == 1, jnp.sum(acc_b, axis=0, keepdims=True), 0.0),
    )
    norm_copies = []
    for g, peers in enumerate(norm_groups):
        if g:
            norm_v[g, 0] = jnp.sum(norm_v[g - 1, 0 : len(norm_groups[g - 1]) + 1], axis=0)
        if not peers:
            continue
        copies = [
            pltpu.make_async_remote_copy(
                src_ref=norm_v.at[g, 0],
                dst_ref=norm_v.at[g, j + 1],
                send_sem=n_send.at[g],
                recv_sem=n_recv.at[g],
                device_id=peer,
                device_id_type=MESH,
            )
            for j, peer in enumerate(peers)
        ]
        for copy in copies:
            copy.start()
        landed = norm_v.at[g, 1 : len(peers) + 1]
        pltpu.make_async_copy(landed, landed, n_recv.at[g]).wait()
        norm_copies.append((g, landed))
    last = len(norm_groups) - 1
    sums = jnp.sum(norm_v[last, 0 : len(norm_groups[last]) + 1], axis=0)
    sums = jnp.sum(sums, axis=1, keepdims=True)
    ratio_ref[...] = jnp.sqrt(sums[0:1] / (sums[1:2] + 1e-6))
    for g, landed in norm_copies:
        pltpu.make_async_copy(landed, landed, n_send.at[g]).wait()

    for copies in (halo1, halo2, halo3, halo4, copies_a, copies_b):
        for copy in copies:
            copy.wait_send()
    store.wait()


def on_device(
    zs,
    xs,
    right_side,
    diag_blocks,
    off_blocks,
    smoother,
    col_index,
    send_list,
    agg_map,
    owner_map,
    coarse_diag,
    coarse_weight,
    coarse_gain,
):
    def rows_of(v):
        return v.reshape(8, 8, 32, 128).transpose(0, 2, 1, 3).reshape(NB * 32, 128)

    off = off_blocks.reshape(NB, KB, 32, 128).transpose(0, 2, 1, 3).reshape(NB * KB * 32, 128)
    hbm = pl.BlockSpec(memory_space=pl.ANY)
    smem = pl.BlockSpec(memory_space=pltpu.SMEM)
    dma = pltpu.SemaphoreType.DMA
    scratch = [
        pltpu.VMEM((TERMS, NB * 64), F32),
        pltpu.VMEM((NB * 32, 128), F32),
        pltpu.VMEM((NB * KB * 32, 128), F32),
        pltpu.VMEM((NB * 32, 128), F32),
        pltpu.VMEM((TILES, 128), jnp.int32),
        pltpu.VMEM((1, NA), jnp.int32),
        pltpu.VMEM((1, NA), F32),
        pltpu.VMEM((1, NA), F32),
        pltpu.VMEM((1, NA), F32),
        pltpu.VMEM((NB, 384, 128), BF16),
        pltpu.VMEM((2, NB + 2 * H, 2, 2 * R1, 128), BF16),
        pltpu.VMEM((TILES, NA, 128), BF16),
        pltpu.VMEM((NB, R, 128), F32),
        pltpu.VMEM((NB, R1, 128), F32),
        pltpu.VMEM((NB, R, 128), F32),
        pltpu.VMEM((NB, R1, 128), F32),
        pltpu.VMEM((TILES, 3 * NOWN, 128), BF16),
        pltpu.VMEM((TILES, 3 * NOWN, 128), BF16),
        pltpu.VMEM((2 * UN, 64, 128), F32),
        pltpu.VMEM((TERMS, NB * 64), F32),
        pltpu.VMEM((2, 2, H // 2, R1, 128), F32),
        pltpu.VMEM((2, 2, H // 2, R1, 128), F32),
        pltpu.VMEM((2, 2, H // 2, R, 128), F32),
        pltpu.VMEM((2, 2, H // 2, R, 128), F32),
        pltpu.VMEM((YC, NOWN, 128), F32),
        pltpu.VMEM((zs, NOWN, 128), F32),
        pltpu.VMEM((2, 64, 8, 128), F32),
        dma((9,)),
        dma((4, 2)),
        dma((4, 2)),
        dma((YC,)),
        dma((YC,)),
        dma((zs,)),
        dma((zs,)),
        dma((2,)),
        dma((2,)),
    ]
    out, ratio = pl.pallas_call(
        functools.partial(kernel, zs, xs),
        out_shape=(
            jax.ShapeDtypeStruct((TERMS, NB * 64), F32),
            jax.ShapeDtypeStruct((1, 1), F32),
        ),
        in_specs=[smem, smem] + [hbm] * 9,
        out_specs=(hbm, pl.BlockSpec(memory_space=pltpu.VMEM)),
        scratch_shapes=scratch,
        compiler_params=pltpu.CompilerParams(
            collective_id=0, has_side_effects=True, vmem_limit_bytes=56 * 1024 * 1024
        ),
    )(
        col_index.T,
        send_list,
        right_side,
        rows_of(diag_blocks),
        off,
        rows_of(smoother),
        agg_map.reshape(TILES, 128),
        owner_map.reshape(1, NA),
        coarse_diag.reshape(1, NA),
        coarse_weight.reshape(1, NA),
        coarse_gain.reshape(1, NA),
    )
    return out, ratio.reshape(())


def solution(mesh):
    placed = (
        P("chaos", "nodes"),
        P("nodes", None),
        P("nodes", None, None),
        P("nodes", None),
        P("nodes", None),
        P("nodes"),
        P("nodes"),
        P("nodes", None),
        P("nodes"),
        P("nodes"),
        P("nodes"),
    )
    return jax.shard_map(
        functools.partial(on_device, mesh.shape["nodes"] // YC, mesh.shape["chaos"]),
        mesh=mesh,
        in_specs=placed,
        out_specs=(P("chaos", "nodes"), P()),
        check_vma=False,
    )
```

```python
import functools
import itertools

import jax
import jax.numpy as jnp
from jax import lax
from jax.experimental import pallas as pl
from jax.experimental.pallas import tpu as pltpu
from jax.sharding import PartitionSpec as P

NB = 64
H = 8
KB = 4
NA = 256
NOWN = 16
TERMS = 30
R = 32
TILES = NB // 2
PAIRS = NB // 4
UN = 32
YC = 8
YS = 4
CS = 2
MESH = pl.DeviceIdType.MESH
F32 = jnp.float32
BF16 = jnp.bfloat16


def dot_nt(a, b, precision=None):
    return lax.dot_general(
        a, b, (((1,), (1,)), ((), ())), precision=precision, preferred_element_type=F32
    )


def dot_nn(a, b):
    return lax.dot_general(a, b, (((1,), (0,)), ((), ())), preferred_element_type=F32)


def split(v):
    hi = v.astype(BF16)
    return hi, (v - hi.astype(F32)).astype(BF16)


def swap(v):
    return pltpu.roll(v, 64, 1)


def kernel(
    zs,
    xs,
    col,
    send_list,
    rhs_hbm,
    diag_hbm,
    off_hbm,
    smooth_hbm,
    agg_hbm,
    owner_hbm,
    cdiag_hbm,
    cweight_hbm,
    cgain_hbm,
    out_hbm,
    ratio_ref,
    rhs_v,
    diag_v,
    off_v,
    smooth_v,
    agg_v,
    owner_v,
    cdiag_v,
    cweight_v,
    cgain_v,
    mats,
    fields,
    owner_fields,
    hot,
    hot_t,
    b_f,
    e_f,
    g_f,
    x_f,
    r_f,
    w_f,
    c_x,
    c_r,
    tmp,
    sol_v,
    snd,
    rcv,
    snd_e,
    rcv_e,
    sum_a,
    sum_b,
    norm_v,
    load_sem,
    halo_send,
    halo_recv,
    a_send,
    a_recv,
    b_send,
    b_recv,
    n_send,
    n_recv,
):
    n = lax.axis_index("nodes")
    x = lax.axis_index("chaos")
    count = zs * YC
    z = n // YC
    yc = n % YC
    y = yc // CS
    c = yc % CS
    right = lax.rem(n + 1, count)
    left = lax.rem(n + count - 1, count)

    def node(zz, yy, cc):
        return (zz * YS + yy) * CS + cc

    loads = [
        pltpu.make_async_copy(src, dst, load_sem.at[i])
        for i, (src, dst) in enumerate(
            [
                (agg_hbm, agg_v),
                (owner_hbm, owner_v),
                (cdiag_hbm, cdiag_v),
                (cweight_hbm, cweight_v),
                (cgain_hbm, cgain_v),
                (smooth_hbm, smooth_v),
                (diag_hbm, diag_v),
                (rhs_hbm, rhs_v),
                (off_hbm, off_v),
            ]
        )
    ]
    for load in loads:
        load.start()

    dims = {"z": zs, "y": YS, "c": CS, "x": xs}
    at = {"z": z, "y": y, "c": c, "x": x}

    def group(axes):
        steps = [offs for offs in itertools.product(*[range(dims[a]) for a in axes]) if any(offs)]
        steps.sort(key=lambda offs: -sum(min(o, dims[a] - o) for a, o in zip(axes, offs)))
        peers = []
        for offs in steps:
            to = dict(at)
            for a, o in zip(axes, offs):
                if o:
                    to[a] = lax.rem(at[a] + o, dims[a])
            peers.append((node(to["z"], to["y"], to["c"]), to["x"]))
        return peers

    peers_a = group("yc")
    peers_b = group("z")

    norm_groups = [group(axes) for axes in ['xy', 'zc']]
    barrier = pltpu.get_barrier_semaphore()
    greeted = [(left, x), (right, x)] + peers_a + peers_b + sum(norm_groups, [])
    for peer in greeted:
        pl.semaphore_signal(barrier, inc=1, device_id=peer, device_id_type=MESH)

    lane = lax.broadcasted_iota(jnp.int32, (1, 128), 1)
    low = lane < 64
    keep_low = low.astype(F32).astype(BF16)
    keep_high = (lane >= 64).astype(F32).astype(BF16)

    def pick(a, b):
        return jnp.where(low, a, b)

    def combine(out, rows):
        u = out[:rows]
        w = u + jnp.where(low, out[rows:], 0.0)
        return w + swap(w)

    def put(store, slot, blk, both, rows):
        hi, lo = split(both)
        store[slot, blk, 0, 0:rows, :] = hi * keep_low
        store[slot, blk, 0, rows : 2 * rows, :] = lo * keep_low
        store[slot, blk, 1, 0:rows, :] = hi * keep_high
        store[slot, blk, 1, rows : 2 * rows, :] = lo * keep_high

    def apply_a(store, slot, blk, rows):
        cols = [col[k, blk] for k in range(KB)]
        near = [
            store[slot, cols[k], 0, 0 : 2 * rows, :] + store[slot, cols[k + 1], 1, 0 : 2 * rows, :]
            for k in (0, 2)
        ]
        own = store[slot, blk, 0, 0 : 2 * rows, :]
        lhs = jnp.concatenate(near + [own], axis=1)
        return combine(dot_nn(lhs, mats[blk]), rows)

    def apply_s(both, blk, rows):
        hi, lo = split(both)
        lhs = jnp.concatenate([hi * keep_high, lo * keep_high], axis=0)
        return combine(dot_nn(lhs, mats[blk, 256:384, :]), rows)

    def halo_copies(stage, src, dst, slot):
        return [
            pltpu.make_async_remote_copy(
                src_ref=src.at[slot, side],
                dst_ref=dst.at[slot, side],
                send_sem=halo_send.at[stage, side],
                recv_sem=halo_recv.at[stage, side],
                device_id=(left if side == 0 else right, x),
                device_id_type=MESH,
            )
            for side in (0, 1)
        ]

    def send_halo(stage, ref, src, dst, slot):
        export_from(ref, src, slot)
        copies = halo_copies(stage, src, dst, slot)
        for copy in copies:
            copy.start()
        return copies

    def take_halo(copies, store, slot, src, rslot, rows):
        for side, base in ((1, NB), (0, NB + H)):
            copies[side].wait_recv()
            for m in range(H // 2):
                tile = src[rslot, side, m]
                other = swap(tile)
                put(store, slot, base + 2 * m, pick(tile, other), rows)
                put(store, slot, base + 2 * m + 1, pick(other, tile), rows)

    def export_from(ref, dst, slot):
        for side in (0, 1):
            for m in range(H // 2):
                first = send_list[side * H + 2 * m]
                second = send_list[side * H + 2 * m + 1]
                dst[slot, side, m] = pick(ref[first], ref[second])

    def loop(body, steps, unroll):
        def step(i, carry):
            body([i * unroll + j for j in range(unroll)])
            return carry

        lax.fori_loop(0, steps // unroll, step, 0)

    def interleave(j, first, second):
        a, b = swap(first), swap(second)
        tmp[j, pl.ds(0, 32, stride=2), :] = pick(first, b)
        tmp[j, pl.ds(1, 32, stride=2), :] = pick(a, second)

    def settle(j, blk, at):
        hi, lo = split(tmp[j])
        mats[blk, at : at + 128, :] = jnp.concatenate([hi, lo], axis=0).T

    def strided8(ref, blk):
        return ref[pl.ds((blk // 8) * 256 + blk % 8, 32, stride=8), :]

    for load in loads[:8]:
        load.wait()

    def prep_own(bs):
        for j, blk in enumerate(bs):
            interleave(j, strided8(diag_v, blk), strided8(smooth_v, blk))
        for j, blk in enumerate(bs):
            settle(j, blk, 256)

    loop(prep_own, NB, UN)

    zero2 = jnp.zeros((2, 128), F32)

    def first_smooth(ts):
        for t in ts:
            tile = rhs_v[:, pl.ds(pl.multiple_of(t * 128, 128), 128)]
            tile = jnp.concatenate([tile, zero2], axis=0)
            other = swap(tile)
            for blk, both in ((2 * t, pick(tile, other)), (2 * t + 1, pick(other, tile))):
                b_f[blk] = both
                step = apply_s(both, blk, R)
                x_f[blk] = step
                put(fields, 0, blk, step, R)

    loop(first_smooth, TILES, 16)

    pl.semaphore_wait(barrier, len(greeted))
    halo1 = send_halo(0, x_f, snd, rcv, 0)

    loads[8].wait()

    def prep_off(bs):
        for j, blk in enumerate(bs):
            parts = [off_v[pl.ds(blk * 128 + k, 32, stride=4), :] for k in range(KB)]
            interleave(2 * j, parts[0], parts[1])
            interleave(2 * j + 1, parts[2], parts[3])
        for j, blk in enumerate(bs):
            settle(2 * j, blk, 0)
            settle(2 * j + 1, blk, 128)

    loop(prep_off, NB, UN)

    take_halo(halo1, fields, 0, rcv, 0, R)

    def second_a(bs):
        out = [b_f[blk] - apply_a(fields, 0, blk, R) for blk in bs]
        for blk, resid in zip(bs, out):
            r_f[blk] = resid

    loop(second_a, NB, UN)

    def second_s(bs):
        done = [x_f[blk] + apply_s(r_f[blk], blk, R) for blk in bs]
        for blk, both in zip(bs, done):
            put(fields, 1, blk, both, R)
            w_f[blk] = both

    loop(second_s, NB, UN)
    halo2 = send_halo(1, w_f, snd, rcv, 1)

    inv = 1.0 / cdiag_v[...]
    gain = cgain_v[...] * inv
    weight = cweight_v[...]
    own_hot = (
        lax.broadcasted_iota(jnp.int32, (NOWN, NA), 0) == owner_v[...]
    ).astype(F32)
    rows_a = lax.broadcasted_iota(jnp.int32, (NA, 256), 0)

    def build_hot(us):
        for u in us:
            line = [agg_v[pl.ds(2 * u + i, 1), :] for i in range(2)]
            one = (rows_a == jnp.concatenate(line, axis=1)).astype(F32).astype(BF16)
            hot[u] = one
            hot_t[u] = one.T

    loop(build_hot, PAIRS, 4)

    g_hi, g_lo = split(own_hot * gain)
    g_lhs = jnp.concatenate([g_hi, g_lo], axis=0)

    def build_pg(us):
        for u in us:
            both = dot_nn(g_lhs, hot[u])
            both = both[:NOWN] + both[NOWN:]
            for i in range(2):
                tile = both[:, 128 * i : 128 * i + 128]
                other = swap(tile)
                for blk, dup in (
                    (4 * u + 2 * i, pick(tile, other)),
                    (4 * u + 2 * i + 1, pick(other, tile)),
                ):
                    e_f[blk] = dup
                    put(owner_fields, 0, blk, dup, NOWN)

    loop(build_pg, PAIRS, 4)
    halo_e1 = send_halo(4, e_f, snd_e, rcv_e, 0)
    take_halo(halo2, fields, 1, rcv, 1, R)

    def triple(tile):
        hi, lo = split(tile)
        return jnp.concatenate([hi, hi, lo], axis=0)

    def resid_all(bs):
        out = [b_f[blk] - apply_a(fields, 1, blk, R) for blk in bs]
        for blk, resid in zip(bs, out):
            r_f[blk] = resid

    loop(resid_all, NB, UN)

    def restrict(i, acc):
        for j in range(8):
            blk = (i * 8 + j) * 4
            tiles = [pick(r_f[blk + 2 * h], r_f[blk + 2 * h + 1]) for h in range(2)]
            hi, lo = split(jnp.concatenate(tiles, axis=1))
            acc = acc + dot_nn(jnp.concatenate([hi, lo], axis=0), hot_t[i * 8 + j])
        return acc

    acc = lax.fori_loop(0, PAIRS // 8, restrict, jnp.zeros((2 * R, NA), F32))
    coarse = (acc[:R] + acc[R:]) * inv
    e_hi, e_lo = split(coarse)
    e_lhs = jnp.concatenate([e_hi, e_lo], axis=0)

    def prolong(us):
        for u in us:
            both = dot_nn(e_lhs, hot[u])
            both = both[:R] + both[R:]
            for i in range(2):
                tile = both[:, 128 * i : 128 * i + 128]
                other = swap(tile)
                for blk, dup in (
                    (4 * u + 2 * i, pick(tile, other)),
                    (4 * u + 2 * i + 1, pick(other, tile)),
                ):
                    b_f[blk] = dup
                    put(fields, 0, blk, dup, R)

    loop(prolong, PAIRS, 4)
    halo3 = send_halo(2, b_f, snd, rcv, 2)

    row = lax.broadcasted_iota(jnp.int32, (R, NA), 0)
    weighted = jnp.where(row == TERMS, gain, coarse) * weight
    part = dot_nt(own_hot, weighted, lax.Precision.HIGHEST)
    sum_a[0] = jnp.concatenate([part, jnp.zeros((NOWN, 128 - R), F32)], axis=1)
    copies_a = [
        pltpu.make_async_remote_copy(
            src_ref=sum_a.at[0],
            dst_ref=sum_a.at[j + 1],
            send_sem=a_send.at[0],
            recv_sem=a_recv.at[0],
            device_id=peer,
            device_id_type=MESH,
        )
        for j, peer in enumerate(peers_a)
    ]
    landed_a = sum_a.at[1 : len(peers_a) + 1]
    for copy in copies_a:
        copy.start()

    take_halo(halo_e1, owner_fields, 0, rcv_e, 0, NOWN)

    def owner_a(bs):
        out = [-apply_a(owner_fields, 0, blk, NOWN) for blk in bs]
        for blk, resid in zip(bs, out):
            g_f[blk] = resid

    loop(owner_a, NB, UN)

    def owner_s(bs):
        done = [e_f[blk] + apply_s(g_f[blk], blk, NOWN) for blk in bs]
        for blk, both in zip(bs, done):
            put(owner_fields, 1, blk, both, NOWN)
            g_f[blk] = both
        for i in range(0, len(bs), 2):
            c_x[bs[i] // 2] = triple(pick(done[i], done[i + 1]))

    loop(owner_s, NB, UN)
    halo_e2 = send_halo(5, g_f, snd_e, rcv_e, 1)

    pltpu.make_async_copy(landed_a, landed_a, a_recv.at[0]).wait()
    sum_b[0] = jnp.sum(sum_a[...], axis=0)
    copies_b = [
        pltpu.make_async_remote_copy(
            src_ref=sum_b.at[0],
            dst_ref=sum_b.at[j + 1],
            send_sem=b_send.at[0],
            recv_sem=b_recv.at[0],
            device_id=peer,
            device_id_type=MESH,
        )
        for j, peer in enumerate(peers_b)
    ]
    landed_b = sum_b.at[1 : len(peers_b) + 1]
    for copy in copies_b:
        copy.start()
    take_halo(halo3, fields, 0, rcv, 2, R)

    def third_a(bs):
        out = [r_f[blk] - apply_a(fields, 0, blk, R) for blk in bs]
        for blk, resid in zip(bs, out):
            x_f[blk] = resid

    loop(third_a, NB, UN)

    def third_s(bs):
        done = [apply_s(x_f[blk], blk, R) for blk in bs]
        for blk, step in zip(bs, done):
            put(fields, 1, blk, step, R)
            r_f[blk] = step

    loop(third_s, NB, UN)
    halo4 = send_halo(3, r_f, snd, rcv, 3)

    take_halo(halo_e2, owner_fields, 1, rcv_e, 1, NOWN)

    def owner_r(bs):
        out = [-apply_a(owner_fields, 1, blk, NOWN) for blk in bs]
        for i in range(0, len(bs), 2):
            c_r[bs[i] // 2] = triple(pick(out[i], out[i + 1]))

    loop(owner_r, NB, UN)

    if peers_b:
        pltpu.make_async_copy(landed_b, landed_b, b_recv.at[0]).wait()
    total = jnp.sum(sum_b[...], axis=0)[:, 0:R]
    total = total * (1.0 + total[:, TERMS : TERMS + 1])
    keep = lax.broadcasted_iota(jnp.int32, (NOWN, R), 1) < TERMS
    s_hi, s_lo = split(jnp.where(keep, total, 0.0).T)
    s_lhs = jnp.concatenate([s_hi, s_lo, s_hi], axis=1)

    def finish(ts):
        for t in ts:
            parts = [b_f[blk] + r_f[blk] + w_f[blk] for blk in (2 * t, 2 * t + 1)]
            tile = pick(parts[0], parts[1]) + dot_nn(s_lhs, c_x[t])
            sol_v[:, pl.ds(pl.multiple_of(t * 128, 128), 128)] = tile[:TERMS]

    loop(finish, TILES, 8)
    store = pltpu.make_async_copy(sol_v, out_hbm, load_sem.at[0])
    store.start()

    take_halo(halo4, fields, 1, rcv, 3, R)

    def final(i, acc):
        for j in range(16):
            t = i * 16 + j
            parts = [x_f[blk] - apply_a(fields, 1, blk, R) for blk in (2 * t, 2 * t + 1)]
            tile = pick(parts[0], parts[1]) + dot_nn(s_lhs, c_r[t])
            acc = acc + tile * tile
        return acc

    acc = lax.fori_loop(0, TILES // 16, final, jnp.zeros((R, 128), F32))

    def right_norm(i, acc):
        tile = rhs_v[:, pl.ds(pl.multiple_of(i * 128, 128), 128)]
        return acc + tile * tile

    acc_b = lax.fori_loop(0, TILES, right_norm, jnp.zeros((TERMS, 128), F32))
    sum_f = jnp.sum(acc, axis=0, keepdims=True)
    sum_r = jnp.sum(acc_b, axis=0, keepdims=True)
    norm_v[0, 0] = pick(sum_f + swap(sum_f), sum_r + swap(sum_r))
    norm_copies = []
    for g, peers in enumerate(norm_groups):
        if g:
            norm_v[g, 0] = jnp.sum(norm_v[g - 1, 0 : len(norm_groups[g - 1]) + 1], axis=0)
        if not peers:
            continue
        copies = [
            pltpu.make_async_remote_copy(
                src_ref=norm_v.at[g, 0],
                dst_ref=norm_v.at[g, j + 1],
                send_sem=n_send.at[g],
                recv_sem=n_recv.at[g],
                device_id=peer,
                device_id_type=MESH,
            )
            for j, peer in enumerate(peers)
        ]
        for copy in copies:
            copy.start()
        if g == 0:
            for sent in (halo1, halo2, halo3, halo4, halo_e1, halo_e2):
                for copy in sent:
                    copy.wait_send()
            pltpu.make_async_copy(landed_a, landed_a, a_send.at[0]).wait()
            if peers_b:
                pltpu.make_async_copy(landed_b, landed_b, b_send.at[0]).wait()
        landed = norm_v.at[g, 1 : len(peers) + 1]
        pltpu.make_async_copy(landed, landed, n_recv.at[g]).wait()
        norm_copies.append((g, landed))
    last = len(norm_groups) - 1
    sums = jnp.sum(norm_v[last, 0 : len(norm_groups[last]) + 1], axis=0)
    sum_f = jnp.sum(jnp.where(low, sums, 0.0), axis=1, keepdims=True)
    sum_r = jnp.sum(jnp.where(low, 0.0, sums), axis=1, keepdims=True)
    ratio_ref[...] = jnp.sqrt(sum_f / (sum_r + 1e-6))
    for g, landed in norm_copies:
        pltpu.make_async_copy(landed, landed, n_send.at[g]).wait()

    store.wait()


def on_device(
    zs,
    xs,
    right_side,
    diag_blocks,
    off_blocks,
    smoother,
    col_index,
    send_list,
    agg_map,
    owner_map,
    coarse_diag,
    coarse_weight,
    coarse_gain,
):
    def rows_of(v):
        return v.reshape(8, 8, 32, 128).transpose(0, 2, 1, 3).reshape(NB * 32, 128)

    off = off_blocks.reshape(NB, KB, 32, 128).transpose(0, 2, 1, 3).reshape(NB * KB * 32, 128)
    hbm = pl.BlockSpec(memory_space=pl.ANY)
    smem = pl.BlockSpec(memory_space=pltpu.SMEM)
    dma = pltpu.SemaphoreType.DMA
    scratch = [
        pltpu.VMEM((TERMS, NB * 64), F32),
        pltpu.VMEM((NB * 32, 128), F32),
        pltpu.VMEM((NB * KB * 32, 128), F32),
        pltpu.VMEM((NB * 32, 128), F32),
        pltpu.VMEM((TILES, 128), jnp.int32),
        pltpu.VMEM((1, NA), jnp.int32),
        pltpu.VMEM((1, NA), F32),
        pltpu.VMEM((1, NA), F32),
        pltpu.VMEM((1, NA), F32),
        pltpu.VMEM((NB, 384, 128), BF16),
        pltpu.VMEM((2, NB + 2 * H, 2, 2 * R, 128), BF16),
        pltpu.VMEM((2, NB + 2 * H, 2, 2 * NOWN, 128), BF16),
        pltpu.VMEM((PAIRS, NA, 256), BF16),
        pltpu.VMEM((PAIRS, 256, NA), BF16),
        pltpu.VMEM((NB, R, 128), F32),
        pltpu.VMEM((NB, NOWN, 128), F32),
        pltpu.VMEM((NB, NOWN, 128), F32),
        pltpu.VMEM((NB, R, 128), F32),
        pltpu.VMEM((NB, R, 128), F32),
        pltpu.VMEM((NB, R, 128), F32),
        pltpu.VMEM((TILES, 3 * NOWN, 128), BF16),
        pltpu.VMEM((TILES, 3 * NOWN, 128), BF16),
        pltpu.VMEM((2 * UN, 64, 128), F32),
        pltpu.VMEM((TERMS, NB * 64), F32),
        pltpu.VMEM((4, 2, H // 2, R, 128), F32),
        pltpu.VMEM((4, 2, H // 2, R, 128), F32),
        pltpu.VMEM((2, 2, H // 2, NOWN, 128), F32),
        pltpu.VMEM((2, 2, H // 2, NOWN, 128), F32),
        pltpu.VMEM((YC, NOWN, 128), F32),
        pltpu.VMEM((zs, NOWN, 128), F32),
        pltpu.VMEM((2, 16, 1, 128), F32),
        dma((9,)),
        dma((6, 2)),
        dma((6, 2)),
        dma((1,)),
        dma((1,)),
        dma((1,)),
        dma((1,)),
        dma((2,)),
        dma((2,)),
    ]
    out, ratio = pl.pallas_call(
        functools.partial(kernel, zs, xs),
        out_shape=(
            jax.ShapeDtypeStruct((TERMS, NB * 64), F32),
            jax.ShapeDtypeStruct((1, 1), F32),
        ),
        in_specs=[smem, smem] + [hbm] * 9,
        out_specs=(hbm, pl.BlockSpec(memory_space=pltpu.VMEM)),
        scratch_shapes=scratch,
        compiler_params=pltpu.CompilerParams(
            collective_id=0, has_side_effects=True, vmem_limit_bytes=56 * 1024 * 1024
        ),
    )(
        col_index.T,
        send_list,
        right_side,
        rows_of(diag_blocks),
        off,
        rows_of(smoother),
        agg_map.reshape(TILES, 128),
        owner_map.reshape(1, NA),
        coarse_diag.reshape(1, NA),
        coarse_weight.reshape(1, NA),
        coarse_gain.reshape(1, NA),
    )
    return out, ratio.reshape(())


def solution(mesh):
    placed = (
        P("chaos", "nodes"),
        P("nodes", None),
        P("nodes", None, None),
        P("nodes", None),
        P("nodes", None),
        P("nodes"),
        P("nodes"),
        P("nodes", None),
        P("nodes"),
        P("nodes"),
        P("nodes"),
    )
    return jax.shard_map(
        functools.partial(on_device, mesh.shape["nodes"] // YC, mesh.shape["chaos"]),
        mesh=mesh,
        in_specs=placed,
        out_specs=(P("chaos", "nodes"), P()),
        check_vma=False,
    )
```

```python
import functools
import itertools

import jax
import jax.numpy as jnp
from jax import lax
from jax.experimental import pallas as pl
from jax.experimental.pallas import tpu as pltpu
from jax.sharding import PartitionSpec as P

NB = 64
H = 8
KB = 4
NA = 256
NOWN = 16
TERMS = 30
R = 32
TILES = NB // 2
PAIRS = NB // 4
UN = 32
YC = 8
YS = 4
CS = 2
MESH = pl.DeviceIdType.MESH
F32 = jnp.float32
BF16 = jnp.bfloat16


def dot_nt(a, b, precision=None):
    return lax.dot_general(
        a, b, (((1,), (1,)), ((), ())), precision=precision, preferred_element_type=F32
    )


def dot_nn(a, b):
    return lax.dot_general(a, b, (((1,), (0,)), ((), ())), preferred_element_type=F32)


def split(v):
    hi = v.astype(BF16)
    return hi, (v - hi.astype(F32)).astype(BF16)


def swap(v):
    return pltpu.roll(v, 64, 1)


def kernel(
    zs,
    xs,
    col,
    send_list,
    rhs_hbm,
    diag_hbm,
    off_hbm,
    smooth_hbm,
    agg_hbm,
    owner_hbm,
    cdiag_hbm,
    cweight_hbm,
    cgain_hbm,
    out_hbm,
    ratio_ref,
    rhs_v,
    diag_v,
    off_v,
    smooth_v,
    agg_v,
    owner_v,
    cdiag_v,
    cweight_v,
    cgain_v,
    mats,
    fields,
    owner_fields,
    hot,
    hot_t,
    b_f,
    e_f,
    g_f,
    x_f,
    r_f,
    w_f,
    c_x,
    c_r,
    tmp,
    sol_v,
    snd,
    rcv,
    snd_e,
    rcv_e,
    sum_a,
    sum_b,
    norm_v,
    load_sem,
    halo_send,
    halo_recv,
    a_send,
    a_recv,
    b_send,
    b_recv,
    n_send,
    n_recv,
):
    n = lax.axis_index("nodes")
    x = lax.axis_index("chaos")
    count = zs * YC
    z = n // YC
    yc = n % YC
    y = yc // CS
    c = yc % CS
    right = lax.rem(n + 1, count)
    left = lax.rem(n + count - 1, count)

    def node(zz, yy, cc):
        return (zz * YS + yy) * CS + cc

    loads = [
        pltpu.make_async_copy(src, dst, load_sem.at[i])
        for i, (src, dst) in enumerate(
            [
                (agg_hbm, agg_v),
                (owner_hbm, owner_v),
                (cdiag_hbm, cdiag_v),
                (cweight_hbm, cweight_v),
                (cgain_hbm, cgain_v),
                (smooth_hbm, smooth_v.at[0 : NB * 32]),
                (diag_hbm, diag_v.at[0 : NB * 32]),
                (rhs_hbm, rhs_v),
                (off_hbm, off_v.at[0 : NB * KB * 32]),
            ]
        )
    ]
    for load in loads:
        load.start()

    dims = {"z": zs, "y": YS, "c": CS, "x": xs}
    at = {"z": z, "y": y, "c": c, "x": x}

    def group(axes):
        steps = [offs for offs in itertools.product(*[range(dims[a]) for a in axes]) if any(offs)]
        steps.sort(key=lambda offs: -sum(min(o, dims[a] - o) for a, o in zip(axes, offs)))
        peers = []
        for offs in steps:
            to = dict(at)
            for a, o in zip(axes, offs):
                if o:
                    to[a] = lax.rem(at[a] + o, dims[a])
            peers.append((node(to["z"], to["y"], to["c"]), to["x"]))
        return peers

    peers_a = group("yc")
    peers_b = group("z")

    norm_groups = [group(axes) for axes in ['xy', 'zc']]
    barrier = pltpu.get_barrier_semaphore()
    greeted = [(left, x), (right, x)] + peers_a + peers_b + sum(norm_groups, [])
    for peer in greeted:
        pl.semaphore_signal(barrier, inc=1, device_id=peer, device_id_type=MESH)

    lane = lax.broadcasted_iota(jnp.int32, (1, 128), 1)
    low = lane < 64
    keep_low = low.astype(F32).astype(BF16)
    keep_high = (lane >= 64).astype(F32).astype(BF16)

    def pick(a, b):
        return jnp.where(low, a, b)

    def combine(out, rows):
        u = out[:rows]
        w = u + jnp.where(low, out[rows:], 0.0)
        return w + swap(w)

    def put(store, slot, blk, both, rows):
        hi, lo = split(both)
        store[slot, blk, 0, 0:rows, :] = hi * keep_low
        store[slot, blk, 0, rows : 2 * rows, :] = lo * keep_low
        store[slot, blk, 1, 0:rows, :] = hi * keep_high
        store[slot, blk, 1, rows : 2 * rows, :] = lo * keep_high

    def apply_a(store, slot, blk, rows):
        cols = [col[k, blk] for k in range(KB)]
        near = [
            store[slot, cols[k], 0, 0 : 2 * rows, :] + store[slot, cols[k + 1], 1, 0 : 2 * rows, :]
            for k in (0, 2)
        ]
        own = store[slot, blk, 0, 0 : 2 * rows, :]
        lhs = jnp.concatenate(near + [own], axis=1)
        return combine(dot_nn(lhs, mats[blk]), rows)

    def apply_s(both, blk, rows):
        hi, lo = split(both)
        lhs = jnp.concatenate([hi * keep_high, lo * keep_high], axis=0)
        return combine(dot_nn(lhs, mats[blk, 256:384, :]), rows)

    def halo_copies(stage, src, dst, slot):
        return [
            pltpu.make_async_remote_copy(
                src_ref=src.at[slot, side],
                dst_ref=dst.at[slot, side],
                send_sem=halo_send.at[stage, side],
                recv_sem=halo_recv.at[stage, side],
                device_id=(left if side == 0 else right, x),
                device_id_type=MESH,
            )
            for side in (0, 1)
        ]

    def send_halo(stage, ref, src, dst, slot):
        export_from(ref, src, slot)
        copies = halo_copies(stage, src, dst, slot)
        for copy in copies:
            copy.start()
        return copies

    def take_halo(copies, store, slot, src, rslot, rows):
        for side, base in ((1, NB), (0, NB + H)):
            copies[side].wait_recv()
            for m in range(H // 2):
                tile = src[rslot, side, m]
                other = swap(tile)
                put(store, slot, base + 2 * m, pick(tile, other), rows)
                put(store, slot, base + 2 * m + 1, pick(other, tile), rows)

    def export_from(ref, dst, slot):
        for side in (0, 1):
            for m in range(H // 2):
                first = send_list[side * H + 2 * m]
                second = send_list[side * H + 2 * m + 1]
                dst[slot, side, m] = pick(ref[first], ref[second])

    def loop(body, steps, unroll):
        def step(i, carry):
            body([i * unroll + j for j in range(unroll)])
            return carry

        lax.fori_loop(0, steps // unroll, step, 0)

    def interleave(j, first, second):
        a, b = swap(first), swap(second)
        tmp[j, pl.ds(0, 32, stride=2), :] = pick(first, b)
        tmp[j, pl.ds(1, 32, stride=2), :] = pick(a, second)

    def settle(j, blk, at):
        hi, lo = split(tmp[j, 0:64])
        mats[blk, at : at + 128, :] = jnp.concatenate([hi, lo], axis=0).T

    def strided8(ref, blk):
        return ref[pl.ds((blk // 8) * 256 + blk % 8, 32, stride=8), :]

    for load in loads[:8]:
        load.wait()

    def prep_own(bs):
        for j, blk in enumerate(bs):
            interleave(j, strided8(diag_v, blk), strided8(smooth_v, blk))
        for j, blk in enumerate(bs):
            settle(j, blk, 256)

    loop(prep_own, NB, UN)

    zero2 = jnp.zeros((2, 128), F32)

    def first_smooth(ts):
        for t in ts:
            tile = rhs_v[:, pl.ds(pl.multiple_of(t * 128, 128), 128)]
            tile = jnp.concatenate([tile, zero2], axis=0)
            other = swap(tile)
            for blk, both in ((2 * t, pick(tile, other)), (2 * t + 1, pick(other, tile))):
                b_f[blk] = both
                step = apply_s(both, blk, R)
                x_f[blk] = step
                put(fields, 0, blk, step, R)

    loop(first_smooth, TILES, 16)

    pl.semaphore_wait(barrier, len(greeted))
    halo1 = send_halo(0, x_f, snd, rcv, 0)

    loads[8].wait()

    def prep_off(bs):
        for j, blk in enumerate(bs):
            parts = [off_v[pl.ds(blk * 128 + k, 32, stride=4), :] for k in range(KB)]
            interleave(2 * j, parts[0], parts[1])
            interleave(2 * j + 1, parts[2], parts[3])
        for j, blk in enumerate(bs):
            settle(2 * j, blk, 0)
            settle(2 * j + 1, blk, 128)

    loop(prep_off, NB, UN)

    take_halo(halo1, fields, 0, rcv, 0, R)

    def second_a(bs):
        out = [b_f[blk] - apply_a(fields, 0, blk, R) for blk in bs]
        for blk, resid in zip(bs, out):
            r_f[blk] = resid

    loop(second_a, NB, UN)

    def second_s(bs):
        done = [x_f[blk] + apply_s(r_f[blk], blk, R) for blk in bs]
        for blk, both in zip(bs, done):
            put(fields, 1, blk, both, R)
            w_f[blk] = both

    loop(second_s, NB, UN)
    halo2 = send_halo(1, w_f, snd, rcv, 1)

    inv = 1.0 / cdiag_v[...]
    gain = cgain_v[...] * inv
    weight = cweight_v[...]
    own_hot = (
        lax.broadcasted_iota(jnp.int32, (NOWN, NA), 0) == owner_v[...]
    ).astype(F32)
    rows_a = lax.broadcasted_iota(jnp.int32, (NA, 256), 0)

    def build_hot(us):
        for u in us:
            line = [agg_v[pl.ds(2 * u + i, 1), :] for i in range(2)]
            one = (rows_a == jnp.concatenate(line, axis=1)).astype(F32).astype(BF16)
            hot[u] = one
            hot_t[u] = one.T

    loop(build_hot, PAIRS, 4)

    g_hi, g_lo = split(own_hot * gain)
    g_lhs = jnp.concatenate([g_hi, g_lo], axis=0)

    def build_pg(us):
        for u in us:
            both = dot_nn(g_lhs, hot[u])
            both = both[:NOWN] + both[NOWN:]
            for i in range(2):
                tile = both[:, 128 * i : 128 * i + 128]
                other = swap(tile)
                for blk, dup in (
                    (4 * u + 2 * i, pick(tile, other)),
                    (4 * u + 2 * i + 1, pick(other, tile)),
                ):
                    e_f[blk] = dup
                    put(owner_fields, 0, blk, dup, NOWN)

    loop(build_pg, PAIRS, 4)
    halo_e1 = send_halo(4, e_f, snd_e, rcv_e, 0)
    take_halo(halo2, fields, 1, rcv, 1, R)

    def triple(tile):
        hi, lo = split(tile)
        return jnp.concatenate([hi, hi, lo], axis=0)

    def resid_all(bs):
        out = [b_f[blk] - apply_a(fields, 1, blk, R) for blk in bs]
        for blk, resid in zip(bs, out):
            r_f[blk] = resid

    loop(resid_all, NB, UN)

    def restrict(i, acc):
        for j in range(8):
            blk = (i * 8 + j) * 4
            tiles = [pick(r_f[blk + 2 * h], r_f[blk + 2 * h + 1]) for h in range(2)]
            hi, lo = split(jnp.concatenate(tiles, axis=1))
            acc = acc + dot_nn(jnp.concatenate([hi, lo], axis=0), hot_t[i * 8 + j])
        return acc

    acc = lax.fori_loop(0, PAIRS // 8, restrict, jnp.zeros((2 * R, NA), F32))
    coarse = (acc[:R] + acc[R:]) * inv
    e_hi, e_lo = split(coarse)
    e_lhs = jnp.concatenate([e_hi, e_lo], axis=0)

    def prolong(us):
        for u in us:
            both = dot_nn(e_lhs, hot[u])
            both = both[:R] + both[R:]
            for i in range(2):
                tile = both[:, 128 * i : 128 * i + 128]
                other = swap(tile)
                for blk, dup in (
                    (4 * u + 2 * i, pick(tile, other)),
                    (4 * u + 2 * i + 1, pick(other, tile)),
                ):
                    b_f[blk] = dup
                    put(fields, 0, blk, dup, R)

    loop(prolong, PAIRS, 4)
    halo3 = send_halo(2, b_f, snd, rcv, 2)

    row = lax.broadcasted_iota(jnp.int32, (R, NA), 0)
    weighted = jnp.where(row == TERMS, gain, coarse) * weight
    part = dot_nt(own_hot, weighted, lax.Precision.HIGHEST)
    sum_a[0] = jnp.concatenate([part, jnp.zeros((NOWN, 128 - R), F32)], axis=1)
    copies_a = [
        pltpu.make_async_remote_copy(
            src_ref=sum_a.at[0],
            dst_ref=sum_a.at[j + 1],
            send_sem=a_send.at[0],
            recv_sem=a_recv.at[0],
            device_id=peer,
            device_id_type=MESH,
        )
        for j, peer in enumerate(peers_a)
    ]
    landed_a = sum_a.at[1 : len(peers_a) + 1]
    for copy in copies_a:
        copy.start()

    take_halo(halo_e1, owner_fields, 0, rcv_e, 0, NOWN)

    def owner_a(bs):
        out = [-apply_a(owner_fields, 0, blk, NOWN) for blk in bs]
        for blk, resid in zip(bs, out):
            g_f[blk] = resid

    loop(owner_a, NB, UN)

    def owner_s(bs):
        done = [e_f[blk] + apply_s(g_f[blk], blk, NOWN) for blk in bs]
        for blk, both in zip(bs, done):
            put(owner_fields, 1, blk, both, NOWN)
            g_f[blk] = both
        for i in range(0, len(bs), 2):
            c_x[bs[i] // 2] = triple(pick(done[i], done[i + 1]))

    loop(owner_s, NB, UN)
    halo_e2 = send_halo(5, g_f, snd_e, rcv_e, 1)

    pltpu.make_async_copy(landed_a, landed_a, a_recv.at[0]).wait()
    sum_b[0] = jnp.sum(sum_a[...], axis=0)
    copies_b = [
        pltpu.make_async_remote_copy(
            src_ref=sum_b.at[0],
            dst_ref=sum_b.at[j + 1],
            send_sem=b_send.at[0],
            recv_sem=b_recv.at[0],
            device_id=peer,
            device_id_type=MESH,
        )
        for j, peer in enumerate(peers_b)
    ]
    landed_b = sum_b.at[1 : len(peers_b) + 1]
    for copy in copies_b:
        copy.start()
    take_halo(halo3, fields, 0, rcv, 2, R)

    def third_a(bs):
        out = [r_f[blk] - apply_a(fields, 0, blk, R) for blk in bs]
        for blk, resid in zip(bs, out):
            x_f[blk] = resid

    loop(third_a, NB, UN)

    def third_s(bs):
        done = [apply_s(x_f[blk], blk, R) for blk in bs]
        for blk, step in zip(bs, done):
            put(fields, 1, blk, step, R)
            r_f[blk] = step

    loop(third_s, NB, UN)
    halo4 = send_halo(3, r_f, snd, rcv, 3)

    take_halo(halo_e2, owner_fields, 1, rcv_e, 1, NOWN)

    def owner_r(bs):
        out = [-apply_a(owner_fields, 1, blk, NOWN) for blk in bs]
        for i in range(0, len(bs), 2):
            c_r[bs[i] // 2] = triple(pick(out[i], out[i + 1]))

    loop(owner_r, NB, UN)

    if peers_b:
        pltpu.make_async_copy(landed_b, landed_b, b_recv.at[0]).wait()
    total = jnp.sum(sum_b[...], axis=0)[:, 0:R]
    total = total * (1.0 + total[:, TERMS : TERMS + 1])
    keep = lax.broadcasted_iota(jnp.int32, (NOWN, R), 1) < TERMS
    s_hi, s_lo = split(jnp.where(keep, total, 0.0).T)
    s_lhs = jnp.concatenate([s_hi, s_lo, s_hi], axis=1)

    def finish(ts):
        for t in ts:
            parts = [b_f[blk] + r_f[blk] + w_f[blk] for blk in (2 * t, 2 * t + 1)]
            tile = pick(parts[0], parts[1]) + dot_nn(s_lhs, c_x[t])
            sol_v[:, pl.ds(pl.multiple_of(t * 128, 128), 128)] = tile[:TERMS]

    loop(finish, TILES, 8)
    store = pltpu.make_async_copy(sol_v, out_hbm, load_sem.at[0])
    store.start()

    take_halo(halo4, fields, 1, rcv, 3, R)

    def final(i, acc):
        for j in range(16):
            t = i * 16 + j
            parts = [x_f[blk] - apply_a(fields, 1, blk, R) for blk in (2 * t, 2 * t + 1)]
            tile = pick(parts[0], parts[1]) + dot_nn(s_lhs, c_r[t])
            acc = acc + tile * tile
        return acc

    acc = lax.fori_loop(0, TILES // 16, final, jnp.zeros((R, 128), F32))

    def right_norm(i, acc):
        tile = rhs_v[:, pl.ds(pl.multiple_of(i * 128, 128), 128)]
        return acc + tile * tile

    acc_b = lax.fori_loop(0, TILES, right_norm, jnp.zeros((TERMS, 128), F32))
    sum_f = jnp.sum(acc, axis=0, keepdims=True)
    sum_r = jnp.sum(acc_b, axis=0, keepdims=True)
    norm_v[0, 0] = pick(sum_f + swap(sum_f), sum_r + swap(sum_r))
    norm_copies = []
    for g, peers in enumerate(norm_groups):
        if g:
            norm_v[g, 0] = jnp.sum(norm_v[g - 1, 0 : len(norm_groups[g - 1]) + 1], axis=0)
        if not peers:
            continue
        copies = [
            pltpu.make_async_remote_copy(
                src_ref=norm_v.at[g, 0],
                dst_ref=norm_v.at[g, j + 1],
                send_sem=n_send.at[g],
                recv_sem=n_recv.at[g],
                device_id=peer,
                device_id_type=MESH,
            )
            for j, peer in enumerate(peers)
        ]
        for copy in copies:
            copy.start()
        if g == 0:
            for sent in (halo1, halo2, halo3, halo4, halo_e1, halo_e2):
                for copy in sent:
                    copy.wait_send()
            pltpu.make_async_copy(landed_a, landed_a, a_send.at[0]).wait()
            if peers_b:
                pltpu.make_async_copy(landed_b, landed_b, b_send.at[0]).wait()
        landed = norm_v.at[g, 1 : len(peers) + 1]
        pltpu.make_async_copy(landed, landed, n_recv.at[g]).wait()
        norm_copies.append((g, landed))
    last = len(norm_groups) - 1
    sums = jnp.sum(norm_v[last, 0 : len(norm_groups[last]) + 1], axis=0)
    sum_f = jnp.sum(jnp.where(low, sums, 0.0), axis=1, keepdims=True)
    sum_r = jnp.sum(jnp.where(low, 0.0, sums), axis=1, keepdims=True)
    ratio_ref[...] = jnp.sqrt(sum_f / (sum_r + 1e-6))
    for g, landed in norm_copies:
        pltpu.make_async_copy(landed, landed, n_send.at[g]).wait()

    store.wait()


def on_device(
    zs,
    xs,
    right_side,
    diag_blocks,
    off_blocks,
    smoother,
    col_index,
    send_list,
    agg_map,
    owner_map,
    coarse_diag,
    coarse_weight,
    coarse_gain,
):
    def rows_of(v):
        return v.reshape(8, 8, 32, 128).transpose(0, 2, 1, 3).reshape(NB * 32, 128)

    off = off_blocks.reshape(NB, KB, 32, 128).transpose(0, 2, 1, 3).reshape(NB * KB * 32, 128)
    hbm = pl.BlockSpec(memory_space=pl.ANY)
    smem = pl.BlockSpec(memory_space=pltpu.SMEM)
    dma = pltpu.SemaphoreType.DMA
    scratch = [
        pltpu.VMEM((TERMS, NB * 64), F32),
        pltpu.VMEM((NB * 32 + 8, 128), F32),
        pltpu.VMEM((NB * KB * 32 + 8, 128), F32),
        pltpu.VMEM((NB * 32 + 8, 128), F32),
        pltpu.VMEM((TILES, 128), jnp.int32),
        pltpu.VMEM((1, NA), jnp.int32),
        pltpu.VMEM((1, NA), F32),
        pltpu.VMEM((1, NA), F32),
        pltpu.VMEM((1, NA), F32),
        pltpu.VMEM((NB, 384, 128), BF16),
        pltpu.VMEM((2, NB + 2 * H, 2, 2 * R, 128), BF16),
        pltpu.VMEM((2, NB + 2 * H, 2, 2 * NOWN, 128), BF16),
        pltpu.VMEM((PAIRS, NA, 256), BF16),
        pltpu.VMEM((PAIRS, 256, NA), BF16),
        pltpu.VMEM((NB, R, 128), F32),
        pltpu.VMEM((NB, NOWN, 128), F32),
        pltpu.VMEM((NB, NOWN, 128), F32),
        pltpu.VMEM((NB, R, 128), F32),
        pltpu.VMEM((NB, R, 128), F32),
        pltpu.VMEM((NB, R, 128), F32),
        pltpu.VMEM((TILES, 3 * NOWN, 128), BF16),
        pltpu.VMEM((TILES, 3 * NOWN, 128), BF16),
        pltpu.VMEM((2 * UN, 72, 128), F32),
        pltpu.VMEM((TERMS, NB * 64), F32),
        pltpu.VMEM((4, 2, H // 2, R, 128), F32),
        pltpu.VMEM((4, 2, H // 2, R, 128), F32),
        pltpu.VMEM((2, 2, H // 2, NOWN, 128), F32),
        pltpu.VMEM((2, 2, H // 2, NOWN, 128), F32),
        pltpu.VMEM((YC, NOWN, 128), F32),
        pltpu.VMEM((zs, NOWN, 128), F32),
        pltpu.VMEM((2, 16, 1, 128), F32),
        dma((9,)),
        dma((6, 2)),
        dma((6, 2)),
        dma((1,)),
        dma((1,)),
        dma((1,)),
        dma((1,)),
        dma((2,)),
        dma((2,)),
    ]
    out, ratio = pl.pallas_call(
        functools.partial(kernel, zs, xs),
        out_shape=(
            jax.ShapeDtypeStruct((TERMS, NB * 64), F32),
            jax.ShapeDtypeStruct((1, 1), F32),
        ),
        in_specs=[smem, smem] + [hbm] * 9,
        out_specs=(hbm, pl.BlockSpec(memory_space=pltpu.VMEM)),
        scratch_shapes=scratch,
        compiler_params=pltpu.CompilerParams(
            collective_id=0, has_side_effects=True, vmem_limit_bytes=56 * 1024 * 1024
        ),
    )(
        col_index.T,
        send_list,
        right_side,
        rows_of(diag_blocks),
        off,
        rows_of(smoother),
        agg_map.reshape(TILES, 128),
        owner_map.reshape(1, NA),
        coarse_diag.reshape(1, NA),
        coarse_weight.reshape(1, NA),
        coarse_gain.reshape(1, NA),
    )
    return out, ratio.reshape(())


def solution(mesh):
    placed = (
        P("chaos", "nodes"),
        P("nodes", None),
        P("nodes", None, None),
        P("nodes", None),
        P("nodes", None),
        P("nodes"),
        P("nodes"),
        P("nodes", None),
        P("nodes"),
        P("nodes"),
        P("nodes"),
    )
    return jax.shard_map(
        functools.partial(on_device, mesh.shape["nodes"] // YC, mesh.shape["chaos"]),
        mesh=mesh,
        in_specs=placed,
        out_specs=(P("chaos", "nodes"), P()),
        check_vma=False,
    )
```
